32 devices in a mesh: tp: 2 (over x), cp: 16 (over z, y, core).
Axes of the slice: x: 2, y: 2, z: 4, core: 2. Of those that a mesh axis runs over, the one named last changes fastest.
Arguments:
- signal: bfloat16 [2048, 4096], P('cp', 'tp'), may hold values from -6 to 6
- cotangent: bfloat16 [2048, 4096], P('cp', 'tp'), may hold values from -0.125 to 0.125
- long_filter: bfloat16 [2048, 2048], P('cp'), may hold values from -6 to 6
Outputs:
- grad_signal: bfloat16 [2048, 4096], P('cp', 'tp')
- grad_filter: bfloat16 [2048, 2048], P('cp')
The draws below stay inside these ranges and needn't reach their ends.
All inputs are finite; a program needn't handle non-finite values.
Results may differ from the reference program's by a relative error of at most 0.0015.
Values may be sent and summed in bfloat16 or wider, within the bound.
No kernel may reach another device: no remote copies, remote signals or barrier semaphores. Data moves between devices by JAX's collectives and lax.ppermute only.
A program may use at most 128 MiB of HBM per device.

```python
import math
import jax
import jax.numpy as jnp
from jax import lax

CHANNELS = 4096
FILTERS = 2048
SEQ = 2048


def shard_levels(rng, extent, shards, smallest, top_value):
    level, own = 1.0, jax.random.fold_in(rng, 6)
    for position, parts in shards:
        steps = jnp.exp(jax.random.uniform(jax.random.fold_in(own, position), (parts,), jnp.float32, smallest / len(shards), top_value / len(shards)))
        level = level * jnp.repeat(steps, extent[position] // parts).reshape([-1 if axis == position else 1 for axis in range(len(extent))])
    return level


def gaussian(key, extent, width, limit, pieces=(), dtype=jnp.bfloat16):
    loudness = shard_levels(key, extent, pieces, -0.22, 0.18) if pieces else 1.0
    array = jax.random.normal(key, extent, jnp.float32) * width * loudness
    return jnp.minimum(jnp.maximum(array, -limit), limit).astype(dtype)


def setup_inputs(seed: int = 0) -> dict:
    seeds = jax.random.split(jax.random.key(seed), 4)
    return {
        "signal": gaussian(seeds[0], (SEQ, CHANNELS), 1.0, 6.0, ((0, 16), (1, 2))),
        "cotangent": gaussian(seeds[1], (SEQ, CHANNELS), (SEQ ** -0.5), 0.125, ((0, 16), (1, 2))),
        "long_filter": gaussian(seeds[2], (SEQ, FILTERS), 1.0, 6.0, ((0, 16),)),
    }


def filter_block(operands):
    sig_block, cot_block, fil_block = operands
    length = 2 * SEQ
    spec_sig = jnp.fft.rfft(sig_block.astype(jnp.float32), n=length, axis=0)
    spec_cot = jnp.fft.rfft(cot_block.astype(jnp.float32), n=length, axis=0)
    spec_fil = jnp.fft.rfft(fil_block.astype(jnp.float32), n=length, axis=0)
    grad_sig = jnp.fft.irfft(jnp.conj(spec_fil)[:, None, :] * spec_cot, n=length, axis=0)[:SEQ]
    summed = jnp.sum(jnp.conj(spec_sig) * spec_cot, axis=1)
    grad_fil = jnp.fft.irfft(summed, n=length, axis=0)[:SEQ]
    return grad_sig.astype(jnp.bfloat16), grad_fil.astype(jnp.bfloat16)


def reference(signal, cotangent, long_filter):
    groups = CHANNELS // FILTERS
    block_cols = math.gcd(FILTERS, 64)
    blocks = FILTERS // block_cols

    def arrange(matrix):
        return matrix.reshape(SEQ, groups, blocks, block_cols).transpose(2, 0, 1, 3)

    filters = long_filter.reshape(SEQ, blocks, block_cols).transpose(1, 0, 2)
    grad_sig, grad_fil = lax.map(filter_block, (arrange(signal), arrange(cotangent), filters))
    grad_signal = grad_sig.transpose(1, 2, 0, 3).reshape(SEQ, CHANNELS)
    grad_filter = grad_fil.transpose(1, 0, 2).reshape(SEQ, FILTERS)
    return grad_signal, grad_filter
```

```python
import functools
import math

import jax
import jax.numpy as jnp
import ml_dtypes
import numpy as np
from jax import lax
from jax.experimental import pallas as pl
from jax.experimental.pallas import tpu as pltpu
from jax.sharding import PartitionSpec as P

LANES = 128
FINE = 128
HALF = LANES // 2
both = ("tp", "cp")


def split(values):
    high = values.astype(ml_dtypes.bfloat16)
    low = (values - high.astype(np.float64)).astype(ml_dtypes.bfloat16)
    return high, low


def tables(coarse):
    total = coarse * FINE
    bins = np.arange(FINE, dtype=np.int64)[None, :, None]
    spots = coarse * np.arange(FINE, dtype=np.int64)[None, None, :] + np.arange(coarse, dtype=np.int64)[:, None, None]
    angle = ((4 * bins + 1) * spots % (4 * total)).astype(np.float64) * (2.0 * math.pi / (4 * total))
    table = np.concatenate([np.cos(angle), -np.sin(angle)], axis=1)
    high, low = split(table)
    forward = np.concatenate([high, low], axis=2)
    high, low = split(table.transpose(0, 2, 1) / total)
    inverse = np.concatenate([high, low, high], axis=2)
    return forward, inverse


def turned(real, imag, turn, size, sign):
    if turn == 0:
        return real, imag
    if 4 * turn == size:
        return (-sign * imag, sign * real) if sign < 0 else (-imag, real)
    if 8 * turn == size or 8 * turn == 3 * size:
        root = math.sqrt(0.5)
        same, cross = (real - sign * imag) * root, (imag + sign * real) * root
        return (same, cross) if 8 * turn == size else (-sign * cross, sign * same)
    cos, sin = math.cos(2 * math.pi * turn / size), sign * math.sin(2 * math.pi * turn / size)
    return real * cos - imag * sin, imag * cos + real * sin


def fourier(data, sign):
    size = len(data)
    if size == 1:
        return data
    even, odd = fourier(data[0::2], sign), fourier(data[1::2], sign)
    low, high = [], []
    for turn in range(size // 2):
        (er, ei), (tr, ti) = even[turn], turned(*odd[turn], turn, size, sign)
        low.append((er + tr, ei + ti))
        high.append((er - tr, ei - ti))
    return low + high


def left_lanes(shape):
    return lax.broadcasted_iota(jnp.int32, shape, 1) < HALF


def merge(left, right):
    return jnp.where(left_lanes(left.shape), left, pltpu.roll(right, HALF, 1))


def merge_right(left, right):
    return jnp.where(left_lanes(left.shape), pltpu.roll(left, HALF, 1), right)


def pack_kernel(part_ref, sig_ref, cot_ref, fil_ref, out_ref):
    rows = sig_ref.shape[0]
    quarter = rows // 4
    part = part_ref[0]
    sig, cot = sig_ref[...].astype(jnp.float32), cot_ref[...].astype(jnp.float32)
    out_ref[0, 0, :rows, :] = merge(sig, cot).astype(jnp.bfloat16)
    out_ref[1, 0, :rows, :] = merge_right(sig, cot).astype(jnp.bfloat16)
    start = pl.multiple_of(part * 2 * quarter, 2 * quarter)
    top = fil_ref[pl.ds(start, quarter), :].astype(jnp.float32)
    bottom = fil_ref[pl.ds(start + quarter, quarter), :].astype(jnp.float32)
    out_ref[0, 0, rows:, :] = merge(top, bottom).astype(jnp.bfloat16)
    out_ref[1, 0, rows:, :] = merge_right(top, bottom).astype(jnp.bfloat16)


def unpack_kernel(in_ref, sig_ref, fil_ref):
    first, second = in_ref[0, 0].astype(jnp.float32), in_ref[1, 0].astype(jnp.float32)
    sig_ref[...] = merge(first, second).astype(jnp.bfloat16)
    fil_ref[...] = merge_right(first, second).astype(jnp.bfloat16)


def gradients(forward_ref, inverse_ref, time_ref, freq_ref, cot_ref):
    coarse = forward_ref.shape[0]

    def onward(index, carry):
        rows = pl.ds(index, FINE, stride=coarse)
        for first, count in ((0, 2), (2, 1)):
            data = jnp.concatenate([time_ref[first + k, rows, :] for k in range(count)], axis=1).astype(jnp.bfloat16)
            bins = jnp.dot(forward_ref[index], jnp.concatenate([data, data], axis=0), preferred_element_type=jnp.float32)
            for k in range(count):
                freq_ref[first + k, index] = bins[:, k * LANES : (k + 1) * LANES]
        return carry

    lax.fori_loop(0, coarse, onward, 0)

    def middle(index, carry):
        real = pl.ds(pl.multiple_of(index * 8, 8), 8)
        imag = pl.ds(pl.multiple_of(index * 8 + FINE, 8), 8)

        def load(which):
            return [(freq_ref[which, c, real, :], freq_ref[which, c, imag, :]) for c in range(coarse)]

        for c, (cr, ci) in enumerate(fourier(load(1), -1)):
            cot_ref[c, real, :] = cr
            cot_ref[c, imag, :] = ci
        for source, target in ((2, 2), (0, 0)):
            products = []
            for c, (br, bi) in enumerate(fourier(load(source), -1)):
                cr, ci = cot_ref[c, real, :], cot_ref[c, imag, :]
                products.append((br * cr + bi * ci, br * ci - bi * cr))
            for c, (pr, pi) in enumerate(fourier(products, 1)):
                freq_ref[target, c, real, :] = pr
                freq_ref[target, c, imag, :] = pi
        return carry

    lax.fori_loop(0, FINE // 8, middle, 0)

    def back(index, carry):
        data = jnp.concatenate([freq_ref[2, index], freq_ref[0, index]], axis=1)
        high = data.astype(jnp.bfloat16)
        low = (data - high.astype(jnp.float32)).astype(jnp.bfloat16)
        values = jnp.dot(
            inverse_ref[index], jnp.concatenate([high, high, low], axis=0), preferred_element_type=jnp.float32
        )
        rows = pl.ds(index, FINE, stride=coarse)
        time_ref[0, rows, :] = values[:, :LANES]
        time_ref[1, rows, :] = values[:, LANES:]
        return carry

    lax.fori_loop(0, coarse, back, 0)


def packed_core(forward_ref, inverse_ref, in_ref, out_ref, time_ref, freq_ref, cot_ref):
    _, places, depth, _ = in_ref.shape
    rows = out_ref.shape[2]
    quarter = rows // 4

    def unfold(place, carry):
        start = pl.multiple_of(place * rows, rows)
        first, second = (in_ref[k, place, :rows, :].astype(jnp.float32) for k in range(2))
        time_ref[0, pl.ds(start, rows), :] = merge(first, second)
        time_ref[1, pl.ds(start, rows), :] = merge_right(first, second)
        for k in range(2):
            fold = in_ref[k, place, rows:, :].astype(jnp.float32)
            time_ref[2, pl.ds(start + 2 * k * quarter, quarter), :] = merge(fold, fold)
            time_ref[2, pl.ds(start + (2 * k + 1) * quarter, quarter), :] = merge_right(fold, fold)
        return carry

    lax.fori_loop(0, places, unfold, 0)
    gradients(forward_ref, inverse_ref, time_ref, freq_ref, cot_ref)

    def fold(place, carry):
        span = pl.ds(pl.multiple_of(place * rows, rows), rows)
        sig, fil = time_ref[0, span, :], time_ref[1, span, :]
        fil = fil + pltpu.roll(fil, HALF, 1)
        left = left_lanes(sig.shape)
        out_ref[0, place] = jnp.where(left, sig, fil).astype(jnp.bfloat16)
        out_ref[1, place] = jnp.where(left, pltpu.roll(sig, HALF, 1), fil).astype(jnp.bfloat16)
        return carry

    lax.fori_loop(0, places, fold, 0)


def plain_core(groups, forward_ref, inverse_ref, in_ref, out_ref, time_ref, freq_ref, cot_ref):
    time_ref[...] = in_ref[...].astype(jnp.float32)
    gradients(forward_ref, inverse_ref, time_ref, freq_ref, cot_ref)
    fil, step = time_ref[1], LANES // groups
    while step < LANES:
        fil, step = fil + pltpu.roll(fil, step, 1), 2 * step
    out_ref[0] = time_ref[0].astype(jnp.bfloat16)
    out_ref[1] = fil.astype(jnp.bfloat16)


def core(kernel, message, out_shape, total):
    coarse = total // FINE
    forward, inverse = tables(coarse)
    return pl.pallas_call(
        kernel,
        out_shape=jax.ShapeDtypeStruct(out_shape, jnp.bfloat16),
        scratch_shapes=[
            pltpu.VMEM((3, total, LANES), jnp.float32),
            pltpu.VMEM((3, coarse, 2 * FINE, LANES), jnp.float32),
            pltpu.VMEM((coarse, 2 * FINE, LANES), jnp.float32),
        ],
        compiler_params=pltpu.CompilerParams(vmem_limit_bytes=60 * 2**20),
        name="gradients",
    )(jnp.asarray(forward), jnp.asarray(inverse), message)


def exchange(message):
    return lax.all_to_all(message, both, split_axis=0, concat_axis=0, tiled=True)


def packed_body(signal, cotangent, long_filter):
    rows, columns = signal.shape
    places = lax.axis_size("cp")
    depth = rows + rows // 4
    column = pl.BlockSpec((rows, LANES), lambda j: (0, j))
    message = pl.pallas_call(
        pack_kernel,
        grid=(places,),
        in_specs=[pl.BlockSpec(memory_space=pltpu.SMEM), column, column, column],
        out_specs=pl.BlockSpec((2, 1, depth, LANES), lambda j: (0, j, 0, 0)),
        out_shape=jax.ShapeDtypeStruct((2, places, depth, LANES), jnp.bfloat16),
        name="pack",
    )(lax.axis_index("tp").reshape(1), signal, cotangent, long_filter)
    message = exchange(message.reshape(2 * places, depth, LANES)).reshape(2, places, depth, LANES)
    message = core(packed_core, message, (2, places, rows, LANES), rows * places)
    message = exchange(message.reshape(2 * places, rows, LANES)).reshape(2, places, rows, LANES)
    return pl.pallas_call(
        unpack_kernel,
        grid=(places,),
        in_specs=[pl.BlockSpec((2, 1, rows, LANES), lambda j: (0, j, 0, 0))],
        out_specs=[column, column],
        out_shape=[jax.ShapeDtypeStruct((rows, columns), jnp.bfloat16)] * 2,
        name="unpack",
    )(message)


def plain_body(signal, cotangent, long_filter):
    rows, columns = signal.shape
    groups, places = lax.axis_size("tp"), lax.axis_size("cp")
    total, width = rows * places, columns // (groups * places)

    def deal(block):
        return block.reshape(block.shape[0], groups * places, width).transpose(1, 0, 2).reshape(groups * places, -1)

    part = lax.axis_index("tp") * (rows // groups)
    share = lax.dynamic_slice_in_dim(long_filter, part, rows // groups, 0)
    message = exchange(jnp.concatenate([deal(signal), deal(cotangent), deal(share)], axis=1))
    sig, cot, fil = jnp.split(message, [rows * width, 2 * rows * width], axis=1)

    def arrange(block):
        block = block.reshape(groups, total, width).transpose(1, 0, 2)
        return jnp.pad(block, ((0, 0), (0, 0), (0, LANES // groups - width))).reshape(total, LANES)

    fil = fil.reshape(groups, places, rows // groups, width).transpose(1, 0, 2, 3).reshape(1, total, width)
    fil = jnp.broadcast_to(fil, (groups, total, width))
    data = jnp.stack([arrange(sig), arrange(cot), arrange(fil)])
    grads = core(functools.partial(plain_core, groups), data, (2, total, LANES), total)
    grads = grads.reshape(2, places, rows, groups, LANES // groups)[..., :width]
    message = exchange(grads.transpose(3, 1, 0, 2, 4).reshape(groups * places, 2 * rows * width))
    grads = message.reshape(groups * places, 2, rows, width).transpose(1, 2, 0, 3).reshape(2, rows, columns)
    return grads[0], grads[1]


def solution(mesh):
    groups, places = mesh.shape["tp"], mesh.shape["cp"]

    def body(signal, cotangent, long_filter):
        rows, columns = signal.shape
        packed = groups == 2 and columns == LANES * places and rows % 64 == 0
        return (packed_body if packed else plain_body)(signal, cotangent, long_filter)

    in_specs = (P("cp", "tp"), P("cp", "tp"), P("cp", None))
    out_specs = (P("cp", "tp"), P("cp", None))
    return jax.shard_map(body, mesh=mesh, in_specs=in_specs, out_specs=out_specs, check_vma=False)
```

```python
import functools
import math

import jax
import jax.numpy as jnp
import ml_dtypes
import numpy as np
from jax import lax
from jax.experimental import pallas as pl
from jax.experimental.pallas import tpu as pltpu
from jax.sharding import PartitionSpec as P

LANES = 128
FINE = 128
HALF = LANES // 2
both = ("tp", "cp")


def split(values):
    high = values.astype(ml_dtypes.bfloat16)
    low = (values - high.astype(np.float64)).astype(ml_dtypes.bfloat16)
    return high, low


def tables(coarse):
    total = coarse * FINE
    bins = np.arange(FINE, dtype=np.int64)[None, :, None]
    spots = coarse * np.arange(FINE, dtype=np.int64)[None, None, :] + np.arange(coarse, dtype=np.int64)[:, None, None]
    angle = ((4 * bins + 1) * spots % (4 * total)).astype(np.float64) * (2.0 * math.pi / (4 * total))
    table = np.concatenate([np.cos(angle), -np.sin(angle)], axis=1)
    high, low = split(table)
    forward = np.concatenate([high, low], axis=2)
    high, low = split(table.transpose(0, 2, 1) / total)
    inverse = np.concatenate([high, low, high], axis=2)
    return forward, inverse


def turned(real, imag, turn, size, sign):
    if turn == 0:
        return real, imag
    if 4 * turn == size:
        return (-sign * imag, sign * real) if sign < 0 else (-imag, real)
    if 8 * turn == size or 8 * turn == 3 * size:
        root = math.sqrt(0.5)
        same, cross = (real - sign * imag) * root, (imag + sign * real) * root
        return (same, cross) if 8 * turn == size else (-sign * cross, sign * same)
    cos, sin = math.cos(2 * math.pi * turn / size), sign * math.sin(2 * math.pi * turn / size)
    return real * cos - imag * sin, imag * cos + real * sin


def fourier(data, sign):
    size = len(data)
    if size == 1:
        return data
    even, odd = fourier(data[0::2], sign), fourier(data[1::2], sign)
    low, high = [], []
    for turn in range(size // 2):
        (er, ei), (tr, ti) = even[turn], turned(*odd[turn], turn, size, sign)
        low.append((er + tr, ei + ti))
        high.append((er - tr, ei - ti))
    return low + high


def left_lanes(shape):
    return lax.broadcasted_iota(jnp.int32, shape, 1) < HALF


def merge(left, right):
    return jnp.where(left_lanes(left.shape), left, pltpu.roll(right, HALF, 1))


def merge_right(left, right):
    return jnp.where(left_lanes(left.shape), pltpu.roll(left, HALF, 1), right)


def pack_kernel(part_ref, sig_ref, cot_ref, fil_ref, out_ref):
    rows = sig_ref.shape[0]
    quarter = rows // 4
    start = pl.multiple_of(part_ref[0] * 2 * quarter, 2 * quarter)
    for place in range(out_ref.shape[1]):
        lanes = pl.ds(place * LANES, LANES)
        sig, cot = sig_ref[:, lanes], cot_ref[:, lanes]
        out_ref[0, place, :rows, :] = merge(sig, cot)
        out_ref[1, place, :rows, :] = merge_right(sig, cot)
        top, bottom = fil_ref[pl.ds(start, quarter), lanes], fil_ref[pl.ds(start + quarter, quarter), lanes]
        out_ref[0, place, rows:, :] = merge(top, bottom)
        out_ref[1, place, rows:, :] = merge_right(top, bottom)


def unpack_kernel(in_ref, sig_ref, fil_ref):
    for place in range(in_ref.shape[1]):
        lanes = pl.ds(place * LANES, LANES)
        first, second = in_ref[0, place], in_ref[1, place]
        sig_ref[:, lanes] = merge(first, second)
        fil_ref[:, lanes] = merge_right(first, second)


def gradients(forward_ref, inverse_ref, time_ref, freq_ref, cot_ref):
    coarse = forward_ref.shape[0]

    def onward(index, carry):
        rows = pl.ds(index, FINE, stride=coarse)
        for first, count in ((0, 2), (2, 1)):
            data = jnp.concatenate([time_ref[first + k, rows, :] for k in range(count)], axis=1).astype(jnp.bfloat16)
            bins = jnp.dot(forward_ref[index], jnp.concatenate([data, data], axis=0), preferred_element_type=jnp.float32)
            for k in range(count):
                freq_ref[first + k, index] = bins[:, k * LANES : (k + 1) * LANES]
        return carry

    lax.fori_loop(0, coarse, onward, 0, unroll=16)

    def middle(index, carry):
        real = pl.ds(pl.multiple_of(index * 8, 8), 8)
        imag = pl.ds(pl.multiple_of(index * 8 + FINE, 8), 8)

        def load(which):
            return [(freq_ref[which, c, real, :], freq_ref[which, c, imag, :]) for c in range(coarse)]

        for c, (cr, ci) in enumerate(fourier(load(1), -1)):
            cot_ref[c, real, :] = cr
            cot_ref[c, imag, :] = ci
        for source, target in ((2, 2), (0, 0)):
            products = []
            for c, (br, bi) in enumerate(fourier(load(source), -1)):
                cr, ci = cot_ref[c, real, :], cot_ref[c, imag, :]
                products.append((br * cr + bi * ci, br * ci - bi * cr))
            for c, (pr, pi) in enumerate(fourier(products, 1)):
                freq_ref[target, c, real, :] = pr
                freq_ref[target, c, imag, :] = pi
        return carry

    lax.fori_loop(0, FINE // 8, middle, 0, unroll=4)

    def back(index, carry):
        data = jnp.concatenate([freq_ref[2, index], freq_ref[0, index]], axis=1)
        high = data.astype(jnp.bfloat16)
        low = (data - high.astype(jnp.float32)).astype(jnp.bfloat16)
        values = jnp.dot(
            inverse_ref[index], jnp.concatenate([high, high, low], axis=0), preferred_element_type=jnp.float32
        )
        rows = pl.ds(index, FINE, stride=coarse)
        time_ref[0, rows, :] = values[:, :LANES]
        time_ref[1, rows, :] = values[:, LANES:]
        return carry

    lax.fori_loop(0, coarse, back, 0, unroll=16)


def packed_core(forward_ref, inverse_ref, in_ref, out_ref, time_ref, freq_ref, cot_ref):
    _, places, depth, _ = in_ref.shape
    rows = out_ref.shape[2]
    quarter = rows // 4

    def unfold(place, carry):
        start = pl.multiple_of(place * rows, rows)
        first, second = (in_ref[k, place, :rows, :].astype(jnp.float32) for k in range(2))
        time_ref[0, pl.ds(start, rows), :] = merge(first, second)
        time_ref[1, pl.ds(start, rows), :] = merge_right(first, second)
        for k in range(2):
            fold = in_ref[k, place, rows:, :].astype(jnp.float32)
            time_ref[2, pl.ds(start + 2 * k * quarter, quarter), :] = merge(fold, fold)
            time_ref[2, pl.ds(start + (2 * k + 1) * quarter, quarter), :] = merge_right(fold, fold)
        return carry

    lax.fori_loop(0, places, unfold, 0, unroll=16)
    gradients(forward_ref, inverse_ref, time_ref, freq_ref, cot_ref)

    def fold(place, carry):
        span = pl.ds(pl.multiple_of(place * rows, rows), rows)
        sig, fil = time_ref[0, span, :], time_ref[1, span, :]
        fil = fil + pltpu.roll(fil, HALF, 1)
        left = left_lanes(sig.shape)
        out_ref[0, place] = jnp.where(left, sig, fil).astype(jnp.bfloat16)
        out_ref[1, place] = jnp.where(left, pltpu.roll(sig, HALF, 1), fil).astype(jnp.bfloat16)
        return carry

    lax.fori_loop(0, places, fold, 0, unroll=16)


def plain_core(groups, forward_ref, inverse_ref, in_ref, out_ref, time_ref, freq_ref, cot_ref):
    time_ref[...] = in_ref[...].astype(jnp.float32)
    gradients(forward_ref, inverse_ref, time_ref, freq_ref, cot_ref)
    fil, step = time_ref[1], LANES // groups
    while step < LANES:
        fil, step = fil + pltpu.roll(fil, step, 1), 2 * step
    out_ref[0] = time_ref[0].astype(jnp.bfloat16)
    out_ref[1] = fil.astype(jnp.bfloat16)


def core(kernel, message, out_shape, total):
    coarse = total // FINE
    forward, inverse = tables(coarse)
    return pl.pallas_call(
        kernel,
        out_shape=jax.ShapeDtypeStruct(out_shape, jnp.bfloat16),
        scratch_shapes=[
            pltpu.VMEM((3, total, LANES), jnp.float32),
            pltpu.VMEM((3, coarse, 2 * FINE, LANES), jnp.float32),
            pltpu.VMEM((coarse, 2 * FINE, LANES), jnp.float32),
        ],
        compiler_params=pltpu.CompilerParams(vmem_limit_bytes=total * 11 * 2**10),
        name="gradients",
    )(jnp.asarray(forward), jnp.asarray(inverse), message)


def exchange(message):
    return lax.all_to_all(message, both, split_axis=0, concat_axis=0, tiled=True)


def packed_body(signal, cotangent, long_filter):
    rows, columns = signal.shape
    places = lax.axis_size("cp")
    depth = rows + rows // 4
    steps = 2
    block = places // steps
    column = pl.BlockSpec((rows, columns // steps), lambda j: (0, j))
    message = pl.pallas_call(
        pack_kernel,
        grid=(steps,),
        in_specs=[pl.BlockSpec(memory_space=pltpu.SMEM), column, column, column],
        out_specs=pl.BlockSpec((2, block, depth, LANES), lambda j: (0, j, 0, 0)),
        out_shape=jax.ShapeDtypeStruct((2, places, depth, LANES), jnp.bfloat16),
        name="pack",
    )(lax.axis_index("tp").reshape(1), signal, cotangent, long_filter)
    message = exchange(message.reshape(2 * places, depth, LANES)).reshape(2, places, depth, LANES)
    message = core(packed_core, message, (2, places, rows, LANES), rows * places)
    message = exchange(message.reshape(2 * places, rows, LANES)).reshape(2, places, rows, LANES)
    return pl.pallas_call(
        unpack_kernel,
        grid=(steps,),
        in_specs=[pl.BlockSpec((2, block, rows, LANES), lambda j: (0, j, 0, 0))],
        out_specs=[column, column],
        out_shape=[jax.ShapeDtypeStruct((rows, columns), jnp.bfloat16)] * 2,
        name="unpack",
    )(message)


def plain_body(signal, cotangent, long_filter):
    rows, columns = signal.shape
    groups, places = lax.axis_size("tp"), lax.axis_size("cp")
    total, width = rows * places, columns // (groups * places)

    def deal(block):
        return block.reshape(block.shape[0], groups * places, width).transpose(1, 0, 2).reshape(groups * places, -1)

    part = lax.axis_index("tp") * (rows // groups)
    share = lax.dynamic_slice_in_dim(long_filter, part, rows // groups, 0)
    message = exchange(jnp.concatenate([deal(signal), deal(cotangent), deal(share)], axis=1))
    sig, cot, fil = jnp.split(message, [rows * width, 2 * rows * width], axis=1)

    def arrange(block):
        block = block.reshape(groups, total, width).transpose(1, 0, 2)
        return jnp.pad(block, ((0, 0), (0, 0), (0, LANES // groups - width))).reshape(total, LANES)

    fil = fil.reshape(groups, places, rows // groups, width).transpose(1, 0, 2, 3).reshape(1, total, width)
    fil = jnp.broadcast_to(fil, (groups, total, width))
    data = jnp.stack([arrange(sig), arrange(cot), arrange(fil)])
    grads = core(functools.partial(plain_core, groups), data, (2, total, LANES), total)
    grads = grads.reshape(2, places, rows, groups, LANES // groups)[..., :width]
    message = exchange(grads.transpose(3, 1, 0, 2, 4).reshape(groups * places, 2 * rows * width))
    grads = message.reshape(groups * places, 2, rows, width).transpose(1, 2, 0, 3).reshape(2, rows, columns)
    return grads[0], grads[1]


def solution(mesh):
    groups, places = mesh.shape["tp"], mesh.shape["cp"]

    def body(signal, cotangent, long_filter):
        rows, columns = signal.shape
        packed = groups == 2 and columns == LANES * places and rows % 64 == 0
        return (packed_body if packed else plain_body)(signal, cotangent, long_filter)

    in_specs = (P("cp", "tp"), P("cp", "tp"), P("cp", None))
    out_specs = (P("cp", "tp"), P("cp", None))
    return jax.shard_map(body, mesh=mesh, in_specs=in_specs, out_specs=out_specs, check_vma=False)
```

```python
import functools
import math

import jax
import jax.numpy as jnp
import ml_dtypes
import numpy as np
from jax import lax
from jax.experimental import pallas as pl
from jax.experimental.pallas import tpu as pltpu
from jax.sharding import PartitionSpec as P

LANES = 128
FINE = 128
HALF = LANES // 2
SLAB = 8
both = ("tp", "cp")


def split(values):
    high = values.astype(ml_dtypes.bfloat16)
    low = (values - high.astype(np.float64)).astype(ml_dtypes.bfloat16)
    return high, low


def tables(coarse):
    total = coarse * FINE
    bins = np.arange(FINE, dtype=np.int64)[None, :, None]
    spots = coarse * np.arange(FINE, dtype=np.int64)[None, None, :] + np.arange(coarse, dtype=np.int64)[:, None, None]
    angle = ((4 * bins + 1) * spots % (4 * total)).astype(np.float64) * (2.0 * math.pi / (4 * total))
    table = np.concatenate([np.cos(angle), -np.sin(angle)], axis=1)
    forward = np.concatenate(split(table), axis=2)
    inverse = np.concatenate(split(table.transpose(0, 2, 1) / total), axis=2)
    return forward, inverse


def butterfly(even, odd, turn, size, sign):
    (er, ei), (dr, di) = even, odd
    if turn == 0:
        return (er + dr, ei + di), (er - dr, ei - di)
    if 4 * turn == size:
        back, forth = (er + di, ei - dr), (er - di, ei + dr)
        return (back, forth) if sign < 0 else (forth, back)
    if 8 * turn in (size, 3 * size):
        root = math.sqrt(0.5)
        total, gap = (dr + di) * root, ((di - dr) if sign < 0 else (dr - di)) * root
        if sign < 0 and 8 * turn == size:
            return (er + total, ei + gap), (er - total, ei - gap)
        if sign < 0:
            return (er + gap, ei - total), (er - gap, ei + total)
        if 8 * turn == size:
            return (er + gap, ei + total), (er - gap, ei - total)
        return (er - total, ei + gap), (er + total, ei - gap)
    cos, sin = math.cos(2 * math.pi * turn / size), sign * math.sin(2 * math.pi * turn / size)
    dr, di = dr * cos - di * sin, di * cos + dr * sin
    return (er + dr, ei + di), (er - dr, ei - di)


def fourier(data, sign):
    size = len(data)
    if size == 1:
        return data
    even, odd = fourier(data[0::2], sign), fourier(data[1::2], sign)
    pairs = [butterfly(even[turn], odd[turn], turn, size, sign) for turn in range(size // 2)]
    return [low for low, _ in pairs] + [high for _, high in pairs]


def left_lanes(shape):
    return lax.broadcasted_iota(jnp.int32, shape, 1) < HALF


def merge(left, right):
    return jnp.where(left_lanes(left.shape), left, pltpu.roll(right, HALF, 1))


def merge_right(left, right):
    return jnp.where(left_lanes(left.shape), pltpu.roll(left, HALF, 1), right)


def pack_kernel(part_ref, sig_ref, cot_ref, fil_ref, out_ref):
    rows = sig_ref.shape[0]
    quarter = rows // 4
    start = pl.multiple_of(part_ref[0] * 2 * quarter, 2 * quarter)
    for place in range(out_ref.shape[1]):
        lanes = pl.ds(place * LANES, LANES)
        sig, cot = sig_ref[:, lanes], cot_ref[:, lanes]
        out_ref[0, place, :rows, :] = merge(sig, cot)
        out_ref[1, place, :rows, :] = merge_right(sig, cot)
        top, bottom = fil_ref[pl.ds(start, quarter), lanes], fil_ref[pl.ds(start + quarter, quarter), lanes]
        out_ref[0, place, rows:, :] = merge(top, bottom)
        out_ref[1, place, rows:, :] = merge_right(top, bottom)


def unpack_kernel(in_ref, sig_ref, fil_ref):
    for place in range(in_ref.shape[1]):
        lanes = pl.ds(place * LANES, LANES)
        first, second = in_ref[0, place], in_ref[1, place]
        sig_ref[:, lanes] = merge(first, second)
        fil_ref[:, lanes] = merge_right(first, second)


def onward(table_ref, time_refs, freq_refs, index):
    rows = pl.ds(index, FINE, stride=table_ref.shape[0])
    data = jnp.concatenate([ref[rows, :] for ref in time_refs], axis=1).astype(jnp.bfloat16)
    data = jnp.concatenate([data, data], axis=0)
    data = jnp.dot(table_ref[index], data, preferred_element_type=jnp.float32)
    for k, ref in enumerate(freq_refs):
        ref[index] = data[:, k * LANES : (k + 1) * LANES]


def back(table_ref, freq_refs, time_refs, index):
    rows = pl.ds(index, FINE, stride=table_ref.shape[0])
    data = jnp.concatenate([ref[index] for ref in freq_refs], axis=1)
    high = data.astype(jnp.bfloat16)
    low = (data - high.astype(jnp.float32)).astype(jnp.bfloat16)
    table = table_ref[index]
    table = jnp.concatenate([table, table[:, : 2 * FINE]], axis=1)
    data = jnp.concatenate([high, high, low], axis=0)
    data = jnp.dot(table, data, preferred_element_type=jnp.float32)
    for k, ref in enumerate(time_refs):
        ref[rows, :] = data[:, k * LANES : (k + 1) * LANES]


def rows_of(index):
    start = pl.multiple_of(index * SLAB, SLAB)
    return pl.ds(start, SLAB), pl.ds(start + FINE, SLAB)


def load(freq_ref, index):
    real, imag = rows_of(index)
    return [(freq_ref[c, real, :], freq_ref[c, imag, :]) for c in range(freq_ref.shape[0])]


def store(freq_ref, index, data):
    real, imag = rows_of(index)
    for c, (dr, di) in enumerate(data):
        freq_ref[c, real, :] = dr
        freq_ref[c, imag, :] = di


def spectrum(freq_ref, index):
    store(freq_ref, index, fourier(load(freq_ref, index), -1))


def correlate(freq_ref, cot_ref, index):
    real, imag = rows_of(index)
    products = []
    for c, (br, bi) in enumerate(fourier(load(freq_ref, index), -1)):
        cr, ci = cot_ref[c, real, :], cot_ref[c, imag, :]
        products.append((br * cr + bi * ci, br * ci - bi * cr))
    store(freq_ref, index, fourier(products, 1))


def each(count, step, unroll):
    def body(index, carry):
        step(index)
        return carry

    lax.fori_loop(0, count, body, 0, unroll=min(unroll, count))


def gradients(forward_ref, inverse_ref, times, freqs, fetch):
    sig_time, cot_time, fil_time = times
    sig_freq, cot_freq, fil_freq = freqs
    coarse = forward_ref.shape[0]

    def beside(matrix, vector, unroll):
        def step(index):
            matrix(index)
            if coarse * SLAB == FINE:
                vector(index)
            else:
                pl.when(index < FINE // SLAB)(lambda: vector(index))

        each(coarse, step, unroll)

    each(coarse, lambda i: onward(forward_ref, (cot_time,), (cot_freq,), i), UNROLL[0])
    beside(
        lambda i: onward(forward_ref, (fil_time, sig_time), (fil_freq, sig_freq), i),
        lambda i: spectrum(cot_freq, i),
        UNROLL[1],
    )
    each(FINE // SLAB, lambda i: correlate(fil_freq, cot_freq, i), UNROLL[2])
    each(FINE // SLAB, lambda i: correlate(sig_freq, cot_freq, i), UNROLL[3])
    fetch.wait()
    each(coarse, lambda i: back(inverse_ref, (sig_freq, fil_freq), (sig_time, fil_time), i), UNROLL[4])


UNROLL = (16, 16, 4, 4, 16)


def packed_core(forward_ref, inverse_hbm, in_ref, out_ref, inverse_ref, arrived, *scratch):
    times, freqs = scratch[:3], scratch[3:]
    _, places, depth, _ = in_ref.shape
    rows = out_ref.shape[2]
    quarter = rows // 4
    fetch = pltpu.make_async_copy(inverse_hbm, inverse_ref, arrived)
    fetch.start()

    def unfold(place):
        start = pl.multiple_of(place * rows, rows)
        first, second = (in_ref[k, place, :rows, :].astype(jnp.float32) for k in range(2))
        times[0][pl.ds(start, rows), :] = merge(first, second)
        times[1][pl.ds(start, rows), :] = merge_right(first, second)
        for k in range(2):
            fold = in_ref[k, place, rows:, :].astype(jnp.float32)
            times[2][pl.ds(start + 2 * k * quarter, quarter), :] = merge(fold, fold)
            times[2][pl.ds(start + (2 * k + 1) * quarter, quarter), :] = merge_right(fold, fold)

    each(places, unfold, 16)
    gradients(forward_ref, inverse_ref, times, freqs, fetch)

    def fold(place):
        span = pl.ds(pl.multiple_of(place * rows, rows), rows)
        sig, fil = times[2][span, :], times[0][span, :]
        fil = fil + pltpu.roll(fil, HALF, 1)
        left = left_lanes(sig.shape)
        out_ref[0, place] = jnp.where(left, sig, fil).astype(jnp.bfloat16)
        out_ref[1, place] = jnp.where(left, pltpu.roll(sig, HALF, 1), fil).astype(jnp.bfloat16)

    each(places, fold, 16)


def plain_core(groups, forward_ref, inverse_hbm, in_ref, out_ref, inverse_ref, arrived, *scratch):
    times, freqs = scratch[:3], scratch[3:]
    fetch = pltpu.make_async_copy(inverse_hbm, inverse_ref, arrived)
    fetch.start()
    for k in range(3):
        times[k][...] = in_ref[k].astype(jnp.float32)
    gradients(forward_ref, inverse_ref, times, freqs, fetch)
    fil, step = times[0][...], LANES // groups
    while step < LANES:
        fil, step = fil + pltpu.roll(fil, step, 1), 2 * step
    out_ref[0] = times[2][...].astype(jnp.bfloat16)
    out_ref[1] = fil.astype(jnp.bfloat16)


def core(kernel, message, out_shape, total):
    coarse = total // FINE
    forward, inverse = tables(coarse)
    vmem = pl.BlockSpec(memory_space=pltpu.VMEM)
    return pl.pallas_call(
        kernel,
        in_specs=[vmem, pl.BlockSpec(memory_space=pltpu.HBM), vmem],
        out_specs=vmem,
        out_shape=pltpu.VMEM(out_shape, jnp.bfloat16),
        scratch_shapes=[pltpu.VMEM(inverse.shape, jnp.bfloat16), pltpu.SemaphoreType.DMA]
        + [pltpu.VMEM((total, LANES), jnp.float32)] * 3
        + [pltpu.VMEM((coarse, 2 * FINE, LANES), jnp.float32)] * 3,
        compiler_params=pltpu.CompilerParams(vmem_limit_bytes=total * 11 * 2**10),
        name="gradients",
    )(jnp.asarray(forward), jnp.asarray(inverse), pltpu.with_memory_space_constraint(message, pltpu.VMEM))


def exchange(message):
    return lax.all_to_all(message, both, split_axis=0, concat_axis=0, tiled=True)


def packed_body(signal, cotangent, long_filter):
    rows, columns = signal.shape
    places = lax.axis_size("cp")
    depth = rows + rows // 4
    steps = 2
    block = places // steps
    column = pl.BlockSpec((rows, columns // steps), lambda j: (0, j))
    message = pl.pallas_call(
        pack_kernel,
        grid=(steps,),
        in_specs=[pl.BlockSpec(memory_space=pltpu.SMEM), column, column, column],
        out_specs=pl.BlockSpec((2, block, depth, LANES), lambda j: (0, j, 0, 0)),
        out_shape=pltpu.VMEM((2, places, depth, LANES), jnp.bfloat16),
        name="pack",
    )(lax.axis_index("tp").reshape(1), signal, cotangent, long_filter)
    message = exchange(message.reshape(2 * places, depth, LANES)).reshape(2, places, depth, LANES)
    message = core(packed_core, message, (2, places, rows, LANES), rows * places)
    message = exchange(message.reshape(2 * places, rows, LANES)).reshape(2, places, rows, LANES)
    return pl.pallas_call(
        unpack_kernel,
        grid=(steps,),
        in_specs=[pl.BlockSpec((2, block, rows, LANES), lambda j: (0, j, 0, 0))],
        out_specs=[column, column],
        out_shape=[jax.ShapeDtypeStruct((rows, columns), jnp.bfloat16)] * 2,
        name="unpack",
    )(pltpu.with_memory_space_constraint(message, pltpu.VMEM))


def plain_body(signal, cotangent, long_filter):
    rows, columns = signal.shape
    groups, places = lax.axis_size("tp"), lax.axis_size("cp")
    total, width = rows * places, columns // (groups * places)

    def deal(block):
        return block.reshape(block.shape[0], groups * places, width).transpose(1, 0, 2).reshape(groups * places, -1)

    part = lax.axis_index("tp") * (rows // groups)
    share = lax.dynamic_slice_in_dim(long_filter, part, rows // groups, 0)
    message = exchange(jnp.concatenate([deal(signal), deal(cotangent), deal(share)], axis=1))
    sig, cot, fil = jnp.split(message, [rows * width, 2 * rows * width], axis=1)

    def arrange(block):
        block = block.reshape(groups, total, width).transpose(1, 0, 2)
        return jnp.pad(block, ((0, 0), (0, 0), (0, LANES // groups - width))).reshape(total, LANES)

    fil = fil.reshape(groups, places, rows // groups, width).transpose(1, 0, 2, 3).reshape(1, total, width)
    fil = jnp.broadcast_to(fil, (groups, total, width))
    data = jnp.stack([arrange(sig), arrange(cot), arrange(fil)])
    grads = core(functools.partial(plain_core, groups), data, (2, total, LANES), total)
    grads = grads.reshape(2, places, rows, groups, LANES // groups)[..., :width]
    message = exchange(grads.transpose(3, 1, 0, 2, 4).reshape(groups * places, 2 * rows * width))
    grads = message.reshape(groups * places, 2, rows, width).transpose(1, 2, 0, 3).reshape(2, rows, columns)
    return grads[0], grads[1]


def solution(mesh):
    groups, places = mesh.shape["tp"], mesh.shape["cp"]

    def body(signal, cotangent, long_filter):
        rows, columns = signal.shape
        packed = groups == 2 and columns == LANES * places and rows % 64 == 0
        return (packed_body if packed else plain_body)(signal, cotangent, long_filter)

    in_specs = (P("cp", "tp"), P("cp", "tp"), P("cp", None))
    out_specs = (P("cp", "tp"), P("cp", None))
    return jax.shard_map(body, mesh=mesh, in_specs=in_specs, out_specs=out_specs, check_vma=False)
```

```python
import functools
import math

import jax
import jax.numpy as jnp
import ml_dtypes
import numpy as np
from jax import lax
from jax.experimental import pallas as pl
from jax.experimental.pallas import tpu as pltpu
from jax.sharding import PartitionSpec as P

LANES = 128
FINE = 128
HALF = LANES // 2
SLAB = 8
IN_CHUNKS = 2
OUT_CHUNKS = 4
both = ("tp", "cp")


def split(values):
    high = values.astype(ml_dtypes.bfloat16)
    low = (values - high.astype(np.float64)).astype(ml_dtypes.bfloat16)
    return high, low


def tables(coarse):
    total = coarse * FINE
    bins = np.arange(FINE, dtype=np.int64)[None, :, None]
    spots = coarse * np.arange(FINE, dtype=np.int64)[None, None, :] + np.arange(coarse, dtype=np.int64)[:, None, None]
    angle = ((4 * bins + 1) * spots % (4 * total)).astype(np.float64) * (2.0 * math.pi / (4 * total))
    table = np.concatenate([np.cos(angle), -np.sin(angle)], axis=1)
    forward = np.concatenate(split(table), axis=2)
    inverse = np.concatenate(split(table.transpose(0, 2, 1) / total), axis=2)
    return forward, inverse


def butterfly(even, odd, turn, size, sign):
    (er, ei), (dr, di) = even, odd
    if turn == 0:
        return (er + dr, ei + di), (er - dr, ei - di)
    if 4 * turn == size:
        back, forth = (er + di, ei - dr), (er - di, ei + dr)
        return (back, forth) if sign < 0 else (forth, back)
    if 8 * turn in (size, 3 * size):
        root = math.sqrt(0.5)
        total, gap = (dr + di) * root, ((di - dr) if sign < 0 else (dr - di)) * root
        if sign < 0 and 8 * turn == size:
            return (er + total, ei + gap), (er - total, ei - gap)
        if sign < 0:
            return (er + gap, ei - total), (er - gap, ei + total)
        if 8 * turn == size:
            return (er + gap, ei + total), (er - gap, ei - total)
        return (er - total, ei + gap), (er + total, ei - gap)
    cos, sin = math.cos(2 * math.pi * turn / size), sign * math.sin(2 * math.pi * turn / size)
    dr, di = dr * cos - di * sin, di * cos + dr * sin
    return (er + dr, ei + di), (er - dr, ei - di)


def fourier(data, sign):
    size = len(data)
    if size == 1:
        return data
    even, odd = fourier(data[0::2], sign), fourier(data[1::2], sign)
    pairs = [butterfly(even[turn], odd[turn], turn, size, sign) for turn in range(size // 2)]
    return [low for low, _ in pairs] + [high for _, high in pairs]


def left_lanes(shape):
    return lax.broadcasted_iota(jnp.int32, shape, 1) < HALF


def merge(left, right):
    return jnp.where(left_lanes(left.shape), left, pltpu.roll(right, HALF, 1))


def merge_right(left, right):
    return jnp.where(left_lanes(left.shape), pltpu.roll(left, HALF, 1), right)


def pack_kernel(part_ref, sig_hbm, cot_hbm, fil_hbm, out_ref, sig_ref, cot_ref, fil_ref, arrived):
    rows, columns = sig_ref.shape
    quarter = rows // 4
    start = pl.multiple_of(part_ref[0] * 2 * quarter, 2 * quarter)
    chunk = columns // IN_CHUNKS
    copies = []
    for c in range(IN_CHUNKS):
        lanes = pl.ds(c * chunk, chunk)
        copies.append(
            (
                pltpu.make_async_copy(sig_hbm.at[:, lanes], sig_ref.at[:, lanes], arrived.at[0, c]),
                pltpu.make_async_copy(cot_hbm.at[:, lanes], cot_ref.at[:, lanes], arrived.at[1, c]),
                pltpu.make_async_copy(
                    fil_hbm.at[pl.ds(start, 2 * quarter), lanes], fil_ref.at[:, lanes], arrived.at[2, c]
                ),
            )
        )
        for copy in copies[c]:
            copy.start()
    for c in range(IN_CHUNKS):
        for copy in copies[c]:
            copy.wait()
        for place in range(c * chunk // LANES, (c + 1) * chunk // LANES):
            lanes = pl.ds(place * LANES, LANES)
            sig, cot = sig_ref[:, lanes], cot_ref[:, lanes]
            out_ref[0, place, :rows, :] = merge(sig, cot)
            out_ref[1, place, :rows, :] = merge_right(sig, cot)
            top, bottom = fil_ref[:quarter, lanes], fil_ref[quarter:, lanes]
            out_ref[0, place, rows:, :] = merge(top, bottom)
            out_ref[1, place, rows:, :] = merge_right(top, bottom)


def unpack_kernel(in_ref, sig_hbm, fil_hbm, sig_ref, fil_ref, sent):
    columns = sig_ref.shape[1]
    chunk = columns // OUT_CHUNKS
    copies = []
    for c in range(OUT_CHUNKS):
        for place in range(c * chunk // LANES, (c + 1) * chunk // LANES):
            lanes = pl.ds(place * LANES, LANES)
            first, second = in_ref[0, place], in_ref[1, place]
            sig_ref[:, lanes] = merge(first, second)
            fil_ref[:, lanes] = merge_right(first, second)
        lanes = pl.ds(c * chunk, chunk)
        copies.append(pltpu.make_async_copy(sig_ref.at[:, lanes], sig_hbm.at[:, lanes], sent.at[0, c]))
        copies.append(pltpu.make_async_copy(fil_ref.at[:, lanes], fil_hbm.at[:, lanes], sent.at[1, c]))
        copies[-2].start()
        copies[-1].start()
    for copy in copies:
        copy.wait()


def pitch(coarse):
    return coarse + 8


def onward(table_ref, time_refs, freq_refs, index):
    rows = pl.ds(index, FINE, stride=pitch(table_ref.shape[0]))
    data = jnp.concatenate([ref[rows, :] for ref in time_refs], axis=1).astype(jnp.bfloat16)
    data = jnp.concatenate([data, data], axis=0)
    data = jnp.dot(table_ref[index], data, preferred_element_type=jnp.float32)
    return [(ref, (index,), data[:, k * LANES : (k + 1) * LANES]) for k, ref in enumerate(freq_refs)]


def back(table_ref, freq_refs, time_refs, finish, index):
    rows = pl.ds(index, FINE, stride=pitch(table_ref.shape[0]))
    data = jnp.concatenate([ref[index] for ref in freq_refs], axis=1)
    high = data.astype(jnp.bfloat16)
    low = (data - high.astype(jnp.float32)).astype(jnp.bfloat16)
    table = table_ref[index]
    table = jnp.concatenate([table, table[:, : 2 * FINE]], axis=1)
    data = jnp.concatenate([high, high, low], axis=0)
    data = jnp.dot(table, data, preferred_element_type=jnp.float32)
    return [(ref, (rows,), part) for ref, part in zip(time_refs, finish(data[:, :LANES], data[:, LANES:]))]


def rows_of(index):
    start = pl.multiple_of(index * SLAB, SLAB)
    return pl.ds(start, SLAB), pl.ds(start + FINE, SLAB)


def load(freq_ref, index):
    real, imag = rows_of(index)
    return [(freq_ref[c, real, :], freq_ref[c, imag, :]) for c in range(freq_ref.shape[0])]


def stores(freq_ref, index, data):
    real, imag = rows_of(index)
    return [(freq_ref, (c, rows), part) for c, pair in enumerate(data) for rows, part in zip((real, imag), pair)]


def spectrum(freq_ref, index):
    return stores(freq_ref, index, fourier(load(freq_ref, index), -1))


def correlate(freq_ref, cot_ref, index):
    data, cot = load(freq_ref, index), load(cot_ref, index)
    products = [
        (br * cr + bi * ci, br * ci - bi * cr) for (br, bi), (cr, ci) in zip(fourier(data, -1), cot)
    ]
    return stores(freq_ref, index, fourier(products, 1))


def each(count, steps, unroll):
    def body(index, carry):
        for ref, where, value in [item for step in steps for item in step(index)]:
            ref[where] = value
        return carry

    lax.fori_loop(0, count, body, 0, unroll=min(unroll, count))


def gradients(forward_ref, inverse_ref, times, freqs, fetch, finish):
    sig_time, cot_time, fil_time = times
    sig_freq, cot_freq, fil_freq = freqs
    coarse, slabs = forward_ref.shape[0], FINE // SLAB

    def beside(matrix, vector, unroll):
        if coarse == slabs:
            each(coarse, (vector, matrix), unroll)
        else:
            each(coarse, (matrix,), unroll)
            each(slabs, (vector,), unroll)

    each(coarse, (lambda i: onward(forward_ref, (cot_time,), (cot_freq,), i),), UNROLL[0])
    beside(
        lambda i: onward(forward_ref, (fil_time, sig_time), (fil_freq, sig_freq), i),
        lambda i: spectrum(cot_freq, i),
        UNROLL[1],
    )
    each(slabs, (lambda i: correlate(fil_freq, cot_freq, i),), UNROLL[2])
    each(slabs, (lambda i: correlate(sig_freq, cot_freq, i),), UNROLL[3])
    fetch.wait()
    each(coarse, (lambda i: back(inverse_ref, (fil_freq, sig_freq), times[:2], finish, i),), UNROLL[4])


UNROLL = (16, 16, 4, 4, 16)


def packed_core(forward_ref, inverse_hbm, in_ref, out_ref, inverse_ref, arrived, *scratch):
    times, freqs = scratch[:3], scratch[3:]
    _, places, depth, _ = in_ref.shape
    rows = out_ref.shape[2]
    fetch = pltpu.make_async_copy(inverse_hbm, inverse_ref, arrived)
    fetch.start()

    coarse = forward_ref.shape[0]
    groups = rows // coarse

    def span(place, group):
        return pl.ds(pl.multiple_of((place * groups + group) * pitch(coarse), 8), coarse)

    def unfold(place):
        first, second = in_ref[0, place, :rows, :], in_ref[1, place, :rows, :]
        folds = [in_ref[k, place, rows:, :] for k in range(2)]
        fil = jnp.concatenate([part for fold in folds for part in (merge(fold, fold), merge_right(fold, fold))], axis=0)
        for ref, data in zip(times, (merge(first, second), merge_right(first, second), fil)):
            data = data.astype(jnp.float32)
            for group in range(groups):
                ref[span(place, group), :] = data[group * coarse : (group + 1) * coarse]
        return ()

    def finish(sig, fil):
        left = left_lanes(sig.shape)
        fil = fil + pltpu.roll(fil, HALF, 1)
        return jnp.where(left, sig, fil), jnp.where(left, pltpu.roll(sig, HALF, 1), fil)

    def fold(place):
        for k in range(2):
            data = jnp.concatenate([times[k][span(place, group), :] for group in range(groups)], axis=0)
            out_ref[k, place] = data.astype(jnp.bfloat16)
        return ()

    each(places, (unfold,), 16)
    gradients(forward_ref, inverse_ref, times, freqs, fetch, finish)
    each(places, (fold,), 16)


def plain_core(groups, forward_ref, inverse_hbm, in_ref, out_ref, inverse_ref, arrived, *scratch):
    times, freqs = scratch[:3], scratch[3:]
    fetch = pltpu.make_async_copy(inverse_hbm, inverse_ref, arrived)
    fetch.start()
    coarse = forward_ref.shape[0]

    def spans(group):
        return (
            pl.ds(pl.multiple_of(group * pitch(coarse), 8), coarse),
            pl.ds(pl.multiple_of(group * coarse, coarse), coarse),
        )

    def unfold(group):
        to, span = spans(group)
        return [(times[k], (to,), in_ref[k, span, :].astype(jnp.float32)) for k in range(3)]

    def finish(sig, fil):
        step = LANES // groups
        while step < LANES:
            fil, step = fil + pltpu.roll(fil, step, 1), 2 * step
        return sig, fil

    def fold(group):
        to, span = spans(group)
        return [(out_ref, (k, span), times[k][to, :].astype(jnp.bfloat16)) for k in range(2)]

    each(FINE, (unfold,), 8)
    gradients(forward_ref, inverse_ref, times, freqs, fetch, finish)
    each(FINE, (fold,), 8)


def core(kernel, message, out_shape, total):
    coarse = total // FINE
    forward, inverse = tables(coarse)
    vmem = pl.BlockSpec(memory_space=pltpu.VMEM)
    return pl.pallas_call(
        kernel,
        in_specs=[vmem, pl.BlockSpec(memory_space=pltpu.HBM), vmem],
        out_specs=vmem,
        out_shape=pltpu.VMEM(out_shape, jnp.bfloat16),
        scratch_shapes=[pltpu.VMEM(inverse.shape, jnp.bfloat16), pltpu.SemaphoreType.DMA]
        + [pltpu.VMEM((FINE * pitch(coarse), LANES), jnp.float32)] * 3
        + [pltpu.VMEM((coarse, 2 * FINE, LANES), jnp.float32)] * 3,
        compiler_params=pltpu.CompilerParams(vmem_limit_bytes=total * 12 * 2**10),
        name="gradients",
    )(jnp.asarray(forward), jnp.asarray(inverse), pltpu.with_memory_space_constraint(message, pltpu.VMEM))


def exchange(message):
    return lax.all_to_all(message, both, split_axis=0, concat_axis=0, tiled=True)


def packed_body(signal, cotangent, long_filter):
    rows, columns = signal.shape
    places = lax.axis_size("cp")
    depth = rows + rows // 4
    hbm, vmem = pl.BlockSpec(memory_space=pltpu.HBM), pl.BlockSpec(memory_space=pltpu.VMEM)
    message = pl.pallas_call(
        pack_kernel,
        in_specs=[pl.BlockSpec(memory_space=pltpu.SMEM), hbm, hbm, hbm],
        out_specs=vmem,
        out_shape=pltpu.VMEM((2, places, depth, LANES), jnp.bfloat16),
        scratch_shapes=[
            pltpu.VMEM((rows, columns), jnp.bfloat16),
            pltpu.VMEM((rows, columns), jnp.bfloat16),
            pltpu.VMEM((rows // 2, columns), jnp.bfloat16),
            pltpu.SemaphoreType.DMA((3, IN_CHUNKS)),
        ],
        name="pack",
    )(lax.axis_index("tp").reshape(1), signal, cotangent, long_filter)
    message = exchange(message.reshape(2 * places, depth, LANES)).reshape(2, places, depth, LANES)
    message = core(packed_core, message, (2, places, rows, LANES), rows * places)
    message = exchange(message.reshape(2 * places, rows, LANES)).reshape(2, places, rows, LANES)
    return pl.pallas_call(
        unpack_kernel,
        in_specs=[vmem],
        out_specs=[hbm, hbm],
        out_shape=[jax.ShapeDtypeStruct((rows, columns), jnp.bfloat16)] * 2,
        scratch_shapes=[pltpu.VMEM((rows, columns), jnp.bfloat16)] * 2 + [pltpu.SemaphoreType.DMA((2, OUT_CHUNKS))],
        name="unpack",
    )(pltpu.with_memory_space_constraint(message, pltpu.VMEM))


def plain_body(signal, cotangent, long_filter):
    rows, columns = signal.shape
    groups, places = lax.axis_size("tp"), lax.axis_size("cp")
    total, width = rows * places, columns // (groups * places)

    def deal(block):
        return block.reshape(block.shape[0], groups * places, width).transpose(1, 0, 2).reshape(groups * places, -1)

    part = lax.axis_index("tp") * (rows // groups)
    share = lax.dynamic_slice_in_dim(long_filter, part, rows // groups, 0)
    message = exchange(jnp.concatenate([deal(signal), deal(cotangent), deal(share)], axis=1))
    sig, cot, fil = jnp.split(message, [rows * width, 2 * rows * width], axis=1)

    def arrange(block):
        block = block.reshape(groups, total, width).transpose(1, 0, 2)
        return jnp.pad(block, ((0, 0), (0, 0), (0, LANES // groups - width))).reshape(total, LANES)

    fil = fil.reshape(groups, places, rows // groups, width).transpose(1, 0, 2, 3).reshape(1, total, width)
    fil = jnp.broadcast_to(fil, (groups, total, width))
    data = jnp.stack([arrange(sig), arrange(cot), arrange(fil)])
    grads = core(functools.partial(plain_core, groups), data, (2, total, LANES), total)
    grads = grads.reshape(2, places, rows, groups, LANES // groups)[..., :width]
    message = exchange(grads.transpose(3, 1, 0, 2, 4).reshape(groups * places, 2 * rows * width))
    grads = message.reshape(groups * places, 2, rows, width).transpose(1, 2, 0, 3).reshape(2, rows, columns)
    return grads[0], grads[1]


def solution(mesh):
    groups, places = mesh.shape["tp"], mesh.shape["cp"]

    def body(signal, cotangent, long_filter):
        rows, columns = signal.shape
        packed = groups == 2 and columns == LANES * places and rows % 64 == 0
        return (packed_body if packed else plain_body)(signal, cotangent, long_filter)

    in_specs = (P("cp", "tp"), P("cp", "tp"), P("cp", None))
    out_specs = (P("cp", "tp"), P("cp", None))
    return jax.shard_map(body, mesh=mesh, in_specs=in_specs, out_specs=out_specs, check_vma=False)
```

```python
import functools
import math

import jax
import jax.numpy as jnp
import ml_dtypes
import numpy as np
from jax import lax
from jax.experimental import pallas as pl
from jax.experimental.pallas import tpu as pltpu
from jax.sharding import PartitionSpec as P

LANES = 128
FINE = 128
HALF = LANES // 2
SLAB = 8
UNROLL = 16
IN_CHUNKS = 2
OUT_CHUNKS = 4
both = ("tp", "cp")


def split(values):
    high = values.astype(ml_dtypes.bfloat16)
    low = (values - high.astype(np.float64)).astype(ml_dtypes.bfloat16)
    return high, low


def tables(coarse):
    total = coarse * FINE
    bins = np.arange(FINE, dtype=np.int64)[None, :, None]
    spots = coarse * np.arange(FINE, dtype=np.int64)[None, None, :] + np.arange(coarse, dtype=np.int64)[:, None, None]
    angle = ((4 * bins + 1) * spots % (4 * total)).astype(np.float64) * (2.0 * math.pi / (4 * total))
    table = np.concatenate([np.cos(angle), -np.sin(angle)], axis=1)
    forward = np.concatenate(split(table), axis=2)
    inverse = np.concatenate(split(table.transpose(0, 2, 1) / total), axis=2)
    return forward, inverse


def butterfly(even, odd, turn, size, sign):
    (er, ei), (dr, di) = even, odd
    if turn == 0:
        return (er + dr, ei + di), (er - dr, ei - di)
    if 4 * turn == size:
        back, forth = (er + di, ei - dr), (er - di, ei + dr)
        return (back, forth) if sign < 0 else (forth, back)
    if 8 * turn in (size, 3 * size):
        root = math.sqrt(0.5)
        total, gap = (dr + di) * root, ((di - dr) if sign < 0 else (dr - di)) * root
        if sign < 0 and 8 * turn == size:
            return (er + total, ei + gap), (er - total, ei - gap)
        if sign < 0:
            return (er + gap, ei - total), (er - gap, ei + total)
        if 8 * turn == size:
            return (er + gap, ei + total), (er - gap, ei - total)
        return (er - total, ei + gap), (er + total, ei - gap)
    cos, sin = math.cos(2 * math.pi * turn / size), sign * math.sin(2 * math.pi * turn / size)
    dr, di = dr * cos - di * sin, di * cos + dr * sin
    return (er + dr, ei + di), (er - dr, ei - di)


def fourier(data, sign):
    size = len(data)
    if size == 1:
        return data
    even, odd = fourier(data[0::2], sign), fourier(data[1::2], sign)
    pairs = [butterfly(even[turn], odd[turn], turn, size, sign) for turn in range(size // 2)]
    return [low for low, _ in pairs] + [high for _, high in pairs]


def left_lanes(shape):
    return lax.broadcasted_iota(jnp.int32, shape, 1) < HALF


def merge(left, right):
    return jnp.where(left_lanes(left.shape), left, pltpu.roll(right, HALF, 1))


def merge_right(left, right):
    return jnp.where(left_lanes(left.shape), pltpu.roll(left, HALF, 1), right)


def pack_kernel(part_ref, sig_hbm, cot_hbm, fil_hbm, out_ref, sig_ref, cot_ref, fil_ref, arrived):
    rows, columns = sig_ref.shape
    quarter = rows // 4
    start = pl.multiple_of(part_ref[0] * 2 * quarter, 2 * quarter)
    chunk = columns // IN_CHUNKS
    copies = []
    for c in range(IN_CHUNKS):
        lanes = pl.ds(c * chunk, chunk)
        copies.append(
            (
                pltpu.make_async_copy(sig_hbm.at[:, lanes], sig_ref.at[:, lanes], arrived.at[0, c]),
                pltpu.make_async_copy(cot_hbm.at[:, lanes], cot_ref.at[:, lanes], arrived.at[1, c]),
                pltpu.make_async_copy(
                    fil_hbm.at[pl.ds(start, 2 * quarter), lanes], fil_ref.at[:, lanes], arrived.at[2, c]
                ),
            )
        )
        for copy in copies[c]:
            copy.start()
    for c in range(IN_CHUNKS):
        for copy in copies[c]:
            copy.wait()
        for place in range(c * chunk // LANES, (c + 1) * chunk // LANES):
            lanes = pl.ds(place * LANES, LANES)
            sig, cot = sig_ref[:, lanes], cot_ref[:, lanes]
            out_ref[0, place, :rows, :] = merge(sig, cot)
            out_ref[1, place, :rows, :] = merge_right(sig, cot)
            top, bottom = fil_ref[:quarter, lanes], fil_ref[quarter:, lanes]
            out_ref[0, place, rows:, :] = merge(top, bottom)
            out_ref[1, place, rows:, :] = merge_right(top, bottom)


def unpack_kernel(in_ref, sig_hbm, fil_hbm, sig_ref, fil_ref, sent):
    columns = sig_ref.shape[1]
    chunk = columns // OUT_CHUNKS
    copies = []
    for c in range(OUT_CHUNKS):
        for place in range(c * chunk // LANES, (c + 1) * chunk // LANES):
            lanes = pl.ds(place * LANES, LANES)
            first, second = in_ref[0, place], in_ref[1, place]
            sig_ref[:, lanes] = merge(first, second)
            fil_ref[:, lanes] = merge_right(first, second)
        lanes = pl.ds(c * chunk, chunk)
        copies.append(pltpu.make_async_copy(sig_ref.at[:, lanes], sig_hbm.at[:, lanes], sent.at[0, c]))
        copies.append(pltpu.make_async_copy(fil_ref.at[:, lanes], fil_hbm.at[:, lanes], sent.at[1, c]))
        copies[-2].start()
        copies[-1].start()
    for copy in copies:
        copy.wait()


def pitch(coarse):
    return coarse + 8


def onward(table_ref, time_refs, freq_refs, index):
    rows = pl.ds(index, FINE, stride=pitch(table_ref.shape[0]))
    data = jnp.concatenate([ref[rows, :] for ref in time_refs], axis=1).astype(jnp.bfloat16)
    data = jnp.concatenate([data, data], axis=0)
    data = jnp.dot(table_ref[index], data, preferred_element_type=jnp.float32)
    return [(ref, (index,), data[:, k * LANES : (k + 1) * LANES]) for k, ref in enumerate(freq_refs)]


def back(table_ref, freq_refs, time_refs, finish, index):
    rows = pl.ds(index, FINE, stride=pitch(table_ref.shape[0]))
    data = jnp.concatenate([ref[index] for ref in freq_refs], axis=1)
    high = data.astype(jnp.bfloat16)
    low = (data - high.astype(jnp.float32)).astype(jnp.bfloat16)
    table = table_ref[index]
    table = jnp.concatenate([table, table[:, : 2 * FINE]], axis=1)
    data = jnp.concatenate([high, high, low], axis=0)
    data = jnp.dot(table, data, preferred_element_type=jnp.float32)
    return [(ref, (rows,), part) for ref, part in zip(time_refs, finish(data[:, :LANES], data[:, LANES:]))]


def rows_of(index):
    start = pl.multiple_of(index * SLAB, SLAB)
    return pl.ds(start, SLAB), pl.ds(start + FINE, SLAB)


def load(freq_ref, index):
    real, imag = rows_of(index)
    return [(freq_ref[c, real, :], freq_ref[c, imag, :]) for c in range(freq_ref.shape[0])]


def stores(freq_ref, index, data):
    real, imag = rows_of(index)
    return [(freq_ref, (c, rows), part) for c, pair in enumerate(data) for rows, part in zip((real, imag), pair)]


def spectrum(freq_ref, index):
    return stores(freq_ref, index, fourier(load(freq_ref, index), -1))


def correlate(freq_ref, cot_ref, index):
    data, cot = load(freq_ref, index), load(cot_ref, index)
    products = [
        (br * cr + bi * ci, br * ci - bi * cr) for (br, bi), (cr, ci) in zip(fourier(data, -1), cot)
    ]
    return stores(freq_ref, index, fourier(products, 1))


def each(count, steps):
    def body(index, carry):
        for ref, where, value in [item for step in steps for item in step(index)]:
            ref[where] = value
        return carry

    lax.fori_loop(0, count, body, 0, unroll=min(UNROLL, count))


def gradients(forward_ref, inverse_ref, times, freqs, fetch, finish):
    sig_time, cot_time, fil_time = times
    sig_freq, cot_freq, fil_freq = freqs
    coarse, slabs = forward_ref.shape[0], FINE // SLAB

    each(coarse, (lambda i: onward(forward_ref, (cot_time, fil_time), (cot_freq, fil_freq), i),))
    each(coarse, (lambda i: onward(forward_ref, (sig_time,), (sig_freq,), i),))
    each(slabs, (lambda i: spectrum(cot_freq, i),))
    each(slabs, (lambda i: correlate(fil_freq, cot_freq, i),))
    each(slabs, (lambda i: correlate(sig_freq, cot_freq, i),))
    fetch.wait()
    each(coarse, (lambda i: back(inverse_ref, (fil_freq, sig_freq), times[:2], finish, i),))


def packed_core(forward_ref, inverse_hbm, in_ref, out_ref, inverse_ref, arrived, *scratch):
    times, freqs = scratch[:3], scratch[3:]
    _, places, depth, _ = in_ref.shape
    rows = out_ref.shape[2]
    fetch = pltpu.make_async_copy(inverse_hbm, inverse_ref, arrived)
    fetch.start()

    coarse = forward_ref.shape[0]
    groups = rows // coarse

    def span(place, group):
        return pl.ds(pl.multiple_of((place * groups + group) * pitch(coarse), 8), coarse)

    def unfold(place):
        first, second = in_ref[0, place, :rows, :], in_ref[1, place, :rows, :]
        folds = [in_ref[k, place, rows:, :] for k in range(2)]
        fil = jnp.concatenate([part for fold in folds for part in (merge(fold, fold), merge_right(fold, fold))], axis=0)
        for ref, data in zip(times, (merge(first, second), merge_right(first, second), fil)):
            data = data.astype(jnp.float32)
            for group in range(groups):
                ref[span(place, group), :] = data[group * coarse : (group + 1) * coarse]
        return ()

    def finish(sig, fil):
        left = left_lanes(sig.shape)
        fil = fil + pltpu.roll(fil, HALF, 1)
        return jnp.where(left, sig, fil), jnp.where(left, pltpu.roll(sig, HALF, 1), fil)

    def fold(place):
        for k in range(2):
            data = jnp.concatenate([times[k][span(place, group), :] for group in range(groups)], axis=0)
            out_ref[k, place] = data.astype(jnp.bfloat16)
        return ()

    each(places, (unfold,))
    gradients(forward_ref, inverse_ref, times, freqs, fetch, finish)
    each(places, (fold,))


def plain_core(groups, forward_ref, inverse_hbm, in_ref, out_ref, inverse_ref, arrived, *scratch):
    times, freqs = scratch[:3], scratch[3:]
    fetch = pltpu.make_async_copy(inverse_hbm, inverse_ref, arrived)
    fetch.start()
    coarse = forward_ref.shape[0]

    def spans(group):
        return (
            pl.ds(pl.multiple_of(group * pitch(coarse), 8), coarse),
            pl.ds(pl.multiple_of(group * coarse, coarse), coarse),
        )

    def unfold(group):
        to, span = spans(group)
        return [(times[k], (to,), in_ref[k, span, :].astype(jnp.float32)) for k in range(3)]

    def finish(sig, fil):
        step = LANES // groups
        while step < LANES:
            fil, step = fil + pltpu.roll(fil, step, 1), 2 * step
        return sig, fil

    def fold(group):
        to, span = spans(group)
        return [(out_ref, (k, span), times[k][to, :].astype(jnp.bfloat16)) for k in range(2)]

    each(FINE, (unfold,))
    gradients(forward_ref, inverse_ref, times, freqs, fetch, finish)
    each(FINE, (fold,))


def core(kernel, message, out_shape, total):
    coarse = total // FINE
    forward, inverse = tables(coarse)
    vmem = pl.BlockSpec(memory_space=pltpu.VMEM)
    return pl.pallas_call(
        kernel,
        in_specs=[vmem, pl.BlockSpec(memory_space=pltpu.HBM), vmem],
        out_specs=vmem,
        out_shape=pltpu.VMEM(out_shape, jnp.bfloat16),
        scratch_shapes=[pltpu.VMEM(inverse.shape, jnp.bfloat16), pltpu.SemaphoreType.DMA]
        + [pltpu.VMEM((FINE * pitch(coarse), LANES), jnp.float32)] * 3
        + [pltpu.VMEM((coarse, 2 * FINE, LANES), jnp.float32)] * 3,
        compiler_params=pltpu.CompilerParams(vmem_limit_bytes=total * 12 * 2**10),
        name="gradients",
    )(jnp.asarray(forward), jnp.asarray(inverse), pltpu.with_memory_space_constraint(message, pltpu.VMEM))


def exchange(message):
    return lax.all_to_all(message, both, split_axis=0, concat_axis=0, tiled=True)


def packed_body(signal, cotangent, long_filter):
    rows, columns = signal.shape
    places = lax.axis_size("cp")
    depth = rows + rows // 4
    hbm, vmem = pl.BlockSpec(memory_space=pltpu.HBM), pl.BlockSpec(memory_space=pltpu.VMEM)
    message = pl.pallas_call(
        pack_kernel,
        in_specs=[pl.BlockSpec(memory_space=pltpu.SMEM), hbm, hbm, hbm],
        out_specs=vmem,
        out_shape=pltpu.VMEM((2, places, depth, LANES), jnp.bfloat16),
        scratch_shapes=[
            pltpu.VMEM((rows, columns), jnp.bfloat16),
            pltpu.VMEM((rows, columns), jnp.bfloat16),
            pltpu.VMEM((rows // 2, columns), jnp.bfloat16),
            pltpu.SemaphoreType.DMA((3, IN_CHUNKS)),
        ],
        name="pack",
    )(lax.axis_index("tp").reshape(1), signal, cotangent, long_filter)
    message = exchange(message.reshape(2 * places, depth, LANES)).reshape(2, places, depth, LANES)
    message = core(packed_core, message, (2, places, rows, LANES), rows * places)
    message = exchange(message.reshape(2 * places, rows, LANES)).reshape(2, places, rows, LANES)
    return pl.pallas_call(
        unpack_kernel,
        in_specs=[vmem],
        out_specs=[hbm, hbm],
        out_shape=[jax.ShapeDtypeStruct((rows, columns), jnp.bfloat16)] * 2,
        scratch_shapes=[pltpu.VMEM((rows, columns), jnp.bfloat16)] * 2 + [pltpu.SemaphoreType.DMA((2, OUT_CHUNKS))],
        name="unpack",
    )(pltpu.with_memory_space_constraint(message, pltpu.VMEM))


def plain_body(signal, cotangent, long_filter):
    rows, columns = signal.shape
    groups, places = lax.axis_size("tp"), lax.axis_size("cp")
    total, width = rows * places, columns // (groups * places)

    def deal(block):
        return block.reshape(block.shape[0], groups * places, width).transpose(1, 0, 2).reshape(groups * places, -1)

    part = lax.axis_index("tp") * (rows // groups)
    share = lax.dynamic_slice_in_dim(long_filter, part, rows // groups, 0)
    message = exchange(jnp.concatenate([deal(signal), deal(cotangent), deal(share)], axis=1))
    sig, cot, fil = jnp.split(message, [rows * width, 2 * rows * width], axis=1)

    def arrange(block):
        block = block.reshape(groups, total, width).transpose(1, 0, 2)
        return jnp.pad(block, ((0, 0), (0, 0), (0, LANES // groups - width))).reshape(total, LANES)

    fil = fil.reshape(groups, places, rows // groups, width).transpose(1, 0, 2, 3).reshape(1, total, width)
    fil = jnp.broadcast_to(fil, (groups, total, width))
    data = jnp.stack([arrange(sig), arrange(cot), arrange(fil)])
    grads = core(functools.partial(plain_core, groups), data, (2, total, LANES), total)
    grads = grads.reshape(2, places, rows, groups, LANES // groups)[..., :width]
    message = exchange(grads.transpose(3, 1, 0, 2, 4).reshape(groups * places, 2 * rows * width))
    grads = message.reshape(groups * places, 2, rows, width).transpose(1, 2, 0, 3).reshape(2, rows, columns)
    return grads[0], grads[1]


def solution(mesh):
    groups, places = mesh.shape["tp"], mesh.shape["cp"]

    def body(signal, cotangent, long_filter):
        rows, columns = signal.shape
        packed = groups == 2 and columns == LANES * places and rows % 64 == 0
        return (packed_body if packed else plain_body)(signal, cotangent, long_filter)

    in_specs = (P("cp", "tp"), P("cp", "tp"), P("cp", None))
    out_specs = (P("cp", "tp"), P("cp", None))
    return jax.shard_map(body, mesh=mesh, in_specs=in_specs, out_specs=out_specs, check_vma=False)
```

```python
import functools
import math

import jax
import jax.numpy as jnp
import ml_dtypes
import numpy as np
from jax import lax
from jax.experimental import pallas as pl
from jax.experimental.pallas import tpu as pltpu
from jax.sharding import PartitionSpec as P

LANES = 128
FINE = 128
HALF = LANES // 2
SLAB = 8
UNROLL = 16
IN_CHUNKS = 2
OUT_CHUNKS = 4
both = ("tp", "cp")


def split(values):
    high = values.astype(ml_dtypes.bfloat16)
    low = (values - high.astype(np.float64)).astype(ml_dtypes.bfloat16)
    return high, low


def tables(coarse):
    total = coarse * FINE
    bins = np.arange(FINE, dtype=np.int64)[None, :, None]
    spots = coarse * np.arange(FINE, dtype=np.int64)[None, None, :] + np.arange(coarse, dtype=np.int64)[:, None, None]
    angle = ((4 * bins + 1) * spots % (4 * total)).astype(np.float64) * (2.0 * math.pi / (4 * total))
    table = np.concatenate([np.cos(angle), -np.sin(angle)], axis=1)
    forward = np.concatenate(split(table), axis=2)
    inverse = np.concatenate(split(table.transpose(0, 2, 1) / total), axis=2)
    return forward, inverse


def butterfly(even, odd, turn, size, sign):
    (er, ei), (dr, di) = even, odd
    if turn == 0:
        return (er + dr, ei + di), (er - dr, ei - di)
    if 4 * turn == size:
        back, forth = (er + di, ei - dr), (er - di, ei + dr)
        return (back, forth) if sign < 0 else (forth, back)
    if 8 * turn in (size, 3 * size):
        root = math.sqrt(0.5)
        total, gap = (dr + di) * root, ((di - dr) if sign < 0 else (dr - di)) * root
        if sign < 0 and 8 * turn == size:
            return (er + total, ei + gap), (er - total, ei - gap)
        if sign < 0:
            return (er + gap, ei - total), (er - gap, ei + total)
        if 8 * turn == size:
            return (er + gap, ei + total), (er - gap, ei - total)
        return (er - total, ei + gap), (er + total, ei - gap)
    cos, sin = math.cos(2 * math.pi * turn / size), sign * math.sin(2 * math.pi * turn / size)
    dr, di = dr * cos - di * sin, di * cos + dr * sin
    return (er + dr, ei + di), (er - dr, ei - di)


def fourier(data, sign):
    size = len(data)
    if size == 1:
        return data
    even, odd = fourier(data[0::2], sign), fourier(data[1::2], sign)
    pairs = [butterfly(even[turn], odd[turn], turn, size, sign) for turn in range(size // 2)]
    return [low for low, _ in pairs] + [high for _, high in pairs]


def left_lanes(shape):
    return lax.broadcasted_iota(jnp.int32, shape, 1) < HALF


def merge(left, right):
    return jnp.where(left_lanes(left.shape), left, pltpu.roll(right, HALF, 1))


def merge_right(left, right):
    return jnp.where(left_lanes(left.shape), pltpu.roll(left, HALF, 1), right)


def pack_kernel(part_ref, sig_hbm, cot_hbm, fil_hbm, out_ref, sig_ref, cot_ref, fil_ref, arrived):
    rows, columns = sig_ref.shape
    quarter = rows // 4
    start = pl.multiple_of(part_ref[0] * 2 * quarter, 2 * quarter)
    chunk = columns // IN_CHUNKS
    copies = []
    for c in range(IN_CHUNKS):
        lanes = pl.ds(c * chunk, chunk)
        copies.append(
            (
                pltpu.make_async_copy(sig_hbm.at[:, lanes], sig_ref.at[:, lanes], arrived.at[0, c]),
                pltpu.make_async_copy(cot_hbm.at[:, lanes], cot_ref.at[:, lanes], arrived.at[1, c]),
                pltpu.make_async_copy(
                    fil_hbm.at[pl.ds(start, 2 * quarter), lanes], fil_ref.at[:, lanes], arrived.at[2, c]
                ),
            )
        )
        for copy in copies[c]:
            copy.start()
    for c in range(IN_CHUNKS):
        for copy in copies[c]:
            copy.wait()
        for place in range(c * chunk // LANES, (c + 1) * chunk // LANES):
            lanes = pl.ds(place * LANES, LANES)
            sig, cot = sig_ref[:, lanes], cot_ref[:, lanes]
            out_ref[0, place, :rows, :] = merge(sig, cot)
            out_ref[1, place, :rows, :] = merge_right(sig, cot)
            top, bottom = fil_ref[:quarter, lanes], fil_ref[quarter:, lanes]
            out_ref[0, place, rows:, :] = merge(top, bottom)
            out_ref[1, place, rows:, :] = merge_right(top, bottom)


def unpack_kernel(in_ref, sig_hbm, fil_hbm, sig_ref, fil_ref, sent):
    columns = sig_ref.shape[1]
    chunk = columns // OUT_CHUNKS
    copies = []
    for c in range(OUT_CHUNKS):
        for place in range(c * chunk // LANES, (c + 1) * chunk // LANES):
            lanes = pl.ds(place * LANES, LANES)
            first, second = in_ref[0, place], in_ref[1, place]
            sig_ref[:, lanes] = merge(first, second)
            fil_ref[:, lanes] = merge_right(first, second)
        lanes = pl.ds(c * chunk, chunk)
        copies.append(pltpu.make_async_copy(sig_ref.at[:, lanes], sig_hbm.at[:, lanes], sent.at[0, c]))
        copies.append(pltpu.make_async_copy(fil_ref.at[:, lanes], fil_hbm.at[:, lanes], sent.at[1, c]))
        copies[-2].start()
        copies[-1].start()
    for copy in copies:
        copy.wait()


def pitch(coarse):
    return coarse + 8


def onward(table_ref, time_refs, freq_refs, index):
    rows = pl.ds(index, FINE, stride=pitch(table_ref.shape[0]))
    data = jnp.concatenate([ref[rows, :] for ref in time_refs], axis=1).astype(jnp.bfloat16)
    data = jnp.concatenate([data, data], axis=0)
    data = jnp.dot(table_ref[index], data, preferred_element_type=jnp.float32)
    return [(ref, (index,), data[:, k * LANES : (k + 1) * LANES]) for k, ref in enumerate(freq_refs)]


def back(table_ref, freq_refs, time_refs, finish, index):
    rows = pl.ds(index, FINE, stride=pitch(table_ref.shape[0]))
    data = jnp.concatenate([ref[index] for ref in freq_refs], axis=1)
    high = data.astype(jnp.bfloat16)
    low = (data - high.astype(jnp.float32)).astype(jnp.bfloat16)
    table = table_ref[index]
    table = jnp.concatenate([table, table[:, : 2 * FINE]], axis=1)
    data = jnp.concatenate([high, high, low], axis=0)
    data = jnp.dot(table, data, preferred_element_type=jnp.float32)
    return [(ref, (rows,), part) for ref, part in zip(time_refs, finish(data[:, :LANES], data[:, LANES:]))]


def rows_of(index):
    start = pl.multiple_of(index * SLAB, SLAB)
    return pl.ds(start, SLAB), pl.ds(start + FINE, SLAB)


def load(freq_ref, index):
    real, imag = rows_of(index)
    return [(freq_ref[c, real, :], freq_ref[c, imag, :]) for c in range(freq_ref.shape[0])]


def stores(freq_ref, index, data):
    real, imag = rows_of(index)
    return [(freq_ref, (c, rows), part) for c, pair in enumerate(data) for rows, part in zip((real, imag), pair)]


def spectrum(freq_ref, index):
    return stores(freq_ref, index, fourier(load(freq_ref, index), -1))


def correlate(freq_ref, cot_ref, index):
    data, cot = load(freq_ref, index), load(cot_ref, index)
    products = [
        (br * cr + bi * ci, br * ci - bi * cr) for (br, bi), (cr, ci) in zip(fourier(data, -1), cot)
    ]
    return stores(freq_ref, index, fourier(products, 1))


def each(count, steps):
    def body(index, carry):
        for ref, where, value in [item for step in steps for item in step(index)]:
            ref[where] = value
        return carry

    lax.fori_loop(0, count, body, 0, unroll=min(UNROLL, count))


def gradients(forward_ref, inverse_ref, times, freqs, fetch, finish):
    sig_time, cot_time, fil_time = times
    sig_freq, cot_freq, fil_freq = freqs
    coarse, slabs = forward_ref.shape[0], FINE // SLAB

    each(coarse, (lambda i: onward(forward_ref, (cot_time, fil_time), (cot_freq, fil_freq), i),))
    each(coarse, (lambda i: onward(forward_ref, (sig_time,), (sig_freq,), i),))
    each(slabs, (lambda i: spectrum(cot_freq, i),))
    each(slabs, (lambda i: correlate(fil_freq, cot_freq, i),))
    each(slabs, (lambda i: correlate(sig_freq, cot_freq, i),))
    fetch.wait()
    each(coarse, (lambda i: back(inverse_ref, (fil_freq, sig_freq), times[:2], finish, i),))


def packed_core(forward_ref, inverse_hbm, in_ref, out_ref, inverse_ref, arrived, *scratch):
    times, freqs = scratch[:3], scratch[3:]
    _, places, depth, _ = in_ref.shape
    rows = out_ref.shape[2]
    fetch = pltpu.make_async_copy(inverse_hbm, inverse_ref, arrived)
    fetch.start()

    coarse = forward_ref.shape[0]
    groups = rows // coarse

    def span(place, group):
        return pl.ds(pl.multiple_of((place * groups + group) * pitch(coarse), 8), coarse)

    def unfold(place):
        first, second = in_ref[0, place, :rows, :], in_ref[1, place, :rows, :]
        folds = [in_ref[k, place, rows:, :] for k in range(2)]
        fil = jnp.concatenate([part for fold in folds for part in (merge(fold, fold), merge_right(fold, fold))], axis=0)
        for ref, data in zip(times, (merge(first, second), merge_right(first, second), fil)):
            data = data.astype(jnp.float32)
            for group in range(groups):
                ref[span(place, group), :] = data[group * coarse : (group + 1) * coarse]
        return ()

    def finish(sig, fil):
        left = left_lanes(sig.shape)
        fil = fil + pltpu.roll(fil, HALF, 1)
        return jnp.where(left, sig, fil), jnp.where(left, pltpu.roll(sig, HALF, 1), fil)

    def fold(place):
        for k in range(2):
            data = jnp.concatenate([times[k][span(place, group), :] for group in range(groups)], axis=0)
            out_ref[k, place] = data.astype(jnp.bfloat16)
        return ()

    each(places, (unfold,))
    gradients(forward_ref, inverse_ref, times, freqs, fetch, finish)
    each(places, (fold,))


def plain_core(groups, forward_ref, inverse_hbm, in_ref, out_ref, inverse_ref, arrived, *scratch):
    times, freqs = scratch[:3], scratch[3:]
    fetch = pltpu.make_async_copy(inverse_hbm, inverse_ref, arrived)
    fetch.start()
    coarse = forward_ref.shape[0]

    def spans(group):
        return (
            pl.ds(pl.multiple_of(group * pitch(coarse), 8), coarse),
            pl.ds(pl.multiple_of(group * coarse, coarse), coarse),
        )

    def unfold(group):
        to, span = spans(group)
        return [(times[k], (to,), in_ref[k, span, :].astype(jnp.float32)) for k in range(3)]

    def finish(sig, fil):
        step = LANES // groups
        while step < LANES:
            fil, step = fil + pltpu.roll(fil, step, 1), 2 * step
        return sig, fil

    def fold(group):
        to, span = spans(group)
        return [(out_ref, (k, span), times[k][to, :].astype(jnp.bfloat16)) for k in range(2)]

    each(FINE, (unfold,))
    gradients(forward_ref, inverse_ref, times, freqs, fetch, finish)
    each(FINE, (fold,))


def core(kernel, message, out_shape, total):
    coarse = total // FINE
    forward, inverse = tables(coarse)
    vmem = pl.BlockSpec(memory_space=pltpu.VMEM)
    return pl.pallas_call(
        kernel,
        in_specs=[vmem, pl.BlockSpec(memory_space=pltpu.HBM), vmem],
        out_specs=vmem,
        out_shape=pltpu.VMEM(out_shape, jnp.bfloat16),
        scratch_shapes=[pltpu.VMEM(inverse.shape, jnp.bfloat16), pltpu.SemaphoreType.DMA]
        + [pltpu.VMEM(((FINE + 1) * pitch(coarse), LANES), jnp.float32)] * 3
        + [pltpu.VMEM((coarse, 2 * FINE, LANES), jnp.float32)] * 3,
        compiler_params=pltpu.CompilerParams(vmem_limit_bytes=total * 12 * 2**10),
        name="gradients",
    )(jnp.asarray(forward), jnp.asarray(inverse), pltpu.with_memory_space_constraint(message, pltpu.VMEM))


def exchange(message):
    return lax.all_to_all(message, both, split_axis=0, concat_axis=0, tiled=True)


def packed_body(signal, cotangent, long_filter):
    rows, columns = signal.shape
    places = lax.axis_size("cp")
    depth = rows + rows // 4
    hbm, vmem = pl.BlockSpec(memory_space=pltpu.HBM), pl.BlockSpec(memory_space=pltpu.VMEM)
    message = pl.pallas_call(
        pack_kernel,
        in_specs=[pl.BlockSpec(memory_space=pltpu.SMEM), hbm, hbm, hbm],
        out_specs=vmem,
        out_shape=pltpu.VMEM((2, places, depth, LANES), jnp.bfloat16),
        scratch_shapes=[
            pltpu.VMEM((rows, columns), jnp.bfloat16),
            pltpu.VMEM((rows, columns), jnp.bfloat16),
            pltpu.VMEM((rows // 2, columns), jnp.bfloat16),
            pltpu.SemaphoreType.DMA((3, IN_CHUNKS)),
        ],
        name="pack",
    )(lax.axis_index("tp").reshape(1), signal, cotangent, long_filter)
    message = exchange(message.reshape(2 * places, depth, LANES)).reshape(2, places, depth, LANES)
    message = core(packed_core, message, (2, places, rows, LANES), rows * places)
    message = exchange(message.reshape(2 * places, rows, LANES)).reshape(2, places, rows, LANES)
    return pl.pallas_call(
        unpack_kernel,
        in_specs=[vmem],
        out_specs=[hbm, hbm],
        out_shape=[jax.ShapeDtypeStruct((rows, columns), jnp.bfloat16)] * 2,
        scratch_shapes=[pltpu.VMEM((rows, columns), jnp.bfloat16)] * 2 + [pltpu.SemaphoreType.DMA((2, OUT_CHUNKS))],
        name="unpack",
    )(pltpu.with_memory_space_constraint(message, pltpu.VMEM))


def plain_body(signal, cotangent, long_filter):
    rows, columns = signal.shape
    groups, places = lax.axis_size("tp"), lax.axis_size("cp")
    total, width = rows * places, columns // (groups * places)

    def deal(block):
        return block.reshape(block.shape[0], groups * places, width).transpose(1, 0, 2).reshape(groups * places, -1)

    part = lax.axis_index("tp") * (rows // groups)
    share = lax.dynamic_slice_in_dim(long_filter, part, rows // groups, 0)
    message = exchange(jnp.concatenate([deal(signal), deal(cotangent), deal(share)], axis=1))
    sig, cot, fil = jnp.split(message, [rows * width, 2 * rows * width], axis=1)

    def arrange(block):
        block = block.reshape(groups, total, width).transpose(1, 0, 2)
        return jnp.pad(block, ((0, 0), (0, 0), (0, LANES // groups - width))).reshape(total, LANES)

    fil = fil.reshape(groups, places, rows // groups, width).transpose(1, 0, 2, 3).reshape(1, total, width)
    fil = jnp.broadcast_to(fil, (groups, total, width))
    data = jnp.stack([arrange(sig), arrange(cot), arrange(fil)])
    grads = core(functools.partial(plain_core, groups), data, (2, total, LANES), total)
    grads = grads.reshape(2, places, rows, groups, LANES // groups)[..., :width]
    message = exchange(grads.transpose(3, 1, 0, 2, 4).reshape(groups * places, 2 * rows * width))
    grads = message.reshape(groups * places, 2, rows, width).transpose(1, 2, 0, 3).reshape(2, rows, columns)
    return grads[0], grads[1]


def solution(mesh):
    groups, places = mesh.shape["tp"], mesh.shape["cp"]

    def body(signal, cotangent, long_filter):
        rows, columns = signal.shape
        packed = groups == 2 and columns == LANES * places and rows % 64 == 0
        return (packed_body if packed else plain_body)(signal, cotangent, long_filter)

    in_specs = (P("cp", "tp"), P("cp", "tp"), P("cp", None))
    out_specs = (P("cp", "tp"), P("cp", None))
    return jax.shard_map(body, mesh=mesh, in_specs=in_specs, out_specs=out_specs, check_vma=False)
```

```python
import functools
import math

import jax
import jax.numpy as jnp
import ml_dtypes
import numpy as np
from jax import lax
from jax.experimental import pallas as pl
from jax.experimental.pallas import tpu as pltpu
from jax.sharding import PartitionSpec as P

LANES = 128
FINE = 128
HALF = LANES // 2
SLAB = 8
UNROLL = 16
IN_CHUNKS = 2
OUT_CHUNKS = 4
both = ("tp", "cp")


def split(values):
    high = values.astype(ml_dtypes.bfloat16)
    low = (values - high.astype(np.float64)).astype(ml_dtypes.bfloat16)
    return high, low


def tables(coarse):
    total = coarse * FINE
    bins = np.arange(FINE, dtype=np.int64)[None, :, None]
    spots = coarse * np.arange(FINE, dtype=np.int64)[None, None, :] + np.arange(coarse, dtype=np.int64)[:, None, None]
    angle = ((4 * bins + 1) * spots % (4 * total)).astype(np.float64) * (2.0 * math.pi / (4 * total))
    table = np.concatenate([np.cos(angle), -np.sin(angle)], axis=1)
    forward = np.concatenate(split(table), axis=2)
    inverse = np.concatenate(split(table.transpose(0, 2, 1) / total), axis=2)
    return forward, inverse


def butterfly(even, odd, turn, size, sign):
    (er, ei), (dr, di) = even, odd
    if turn == 0:
        return (er + dr, ei + di), (er - dr, ei - di)
    if 4 * turn == size:
        back, forth = (er + di, ei - dr), (er - di, ei + dr)
        return (back, forth) if sign < 0 else (forth, back)
    if 8 * turn in (size, 3 * size):
        root = math.sqrt(0.5)
        total, gap = (dr + di) * root, ((di - dr) if sign < 0 else (dr - di)) * root
        if sign < 0 and 8 * turn == size:
            return (er + total, ei + gap), (er - total, ei - gap)
        if sign < 0:
            return (er + gap, ei - total), (er - gap, ei + total)
        if 8 * turn == size:
            return (er + gap, ei + total), (er - gap, ei - total)
        return (er - total, ei + gap), (er + total, ei - gap)
    cos, sin = math.cos(2 * math.pi * turn / size), sign * math.sin(2 * math.pi * turn / size)
    dr, di = dr * cos - di * sin, di * cos + dr * sin
    return (er + dr, ei + di), (er - dr, ei - di)


def fourier(data, sign):
    size = len(data)
    if size == 1:
        return data
    even, odd = fourier(data[0::2], sign), fourier(data[1::2], sign)
    pairs = [butterfly(even[turn], odd[turn], turn, size, sign) for turn in range(size // 2)]
    return [low for low, _ in pairs] + [high for _, high in pairs]


def left_lanes(shape):
    return lax.broadcasted_iota(jnp.int32, shape, 1) < HALF


def merge(left, right):
    return jnp.where(left_lanes(left.shape), left, pltpu.roll(right, HALF, 1))


def merge_right(left, right):
    return jnp.where(left_lanes(left.shape), pltpu.roll(left, HALF, 1), right)


def pack_kernel(part_ref, sig_hbm, cot_hbm, fil_hbm, out_ref, sig_ref, cot_ref, fil_ref, arrived):
    rows, columns = sig_ref.shape
    quarter = rows // 4
    start = pl.multiple_of(part_ref[0] * 2 * quarter, 2 * quarter)
    chunk = columns // IN_CHUNKS
    copies = []
    for c in range(IN_CHUNKS):
        lanes = pl.ds(c * chunk, chunk)
        copies.append(
            (
                pltpu.make_async_copy(sig_hbm.at[:, lanes], sig_ref.at[:, lanes], arrived.at[0, c]),
                pltpu.make_async_copy(cot_hbm.at[:, lanes], cot_ref.at[:, lanes], arrived.at[1, c]),
                pltpu.make_async_copy(
                    fil_hbm.at[pl.ds(start, 2 * quarter), lanes], fil_ref.at[:, lanes], arrived.at[2, c]
                ),
            )
        )
        for copy in copies[c]:
            copy.start()
    for c in range(IN_CHUNKS):
        for copy in copies[c]:
            copy.wait()
        for place in range(c * chunk // LANES, (c + 1) * chunk // LANES):
            lanes = pl.ds(place * LANES, LANES)
            sig, cot = sig_ref[:, lanes], cot_ref[:, lanes]
            out_ref[0, place, :rows, :] = merge(sig, cot)
            out_ref[1, place, :rows, :] = merge_right(sig, cot)
            top, bottom = fil_ref[:quarter, lanes], fil_ref[quarter:, lanes]
            out_ref[0, place, rows:, :] = merge(top, bottom)
            out_ref[1, place, rows:, :] = merge_right(top, bottom)


def unpack_kernel(in_ref, sig_hbm, fil_hbm, sig_ref, fil_ref, sent):
    columns = sig_ref.shape[1]
    chunk = columns // OUT_CHUNKS
    copies = []
    for c in range(OUT_CHUNKS):
        for place in range(c * chunk // LANES, (c + 1) * chunk // LANES):
            lanes = pl.ds(place * LANES, LANES)
            first, second = in_ref[0, place], in_ref[1, place]
            sig_ref[:, lanes] = merge(first, second)
            fil_ref[:, lanes] = merge_right(first, second)
        lanes = pl.ds(c * chunk, chunk)
        copies.append(pltpu.make_async_copy(sig_ref.at[:, lanes], sig_hbm.at[:, lanes], sent.at[0, c]))
        copies.append(pltpu.make_async_copy(fil_ref.at[:, lanes], fil_hbm.at[:, lanes], sent.at[1, c]))
        copies[-2].start()
        copies[-1].start()
    for copy in copies:
        copy.wait()


def pitch(coarse):
    return coarse + 8


def onward(table_ref, time_refs, freq_refs, index):
    rows = pl.ds(index, FINE, stride=pitch(table_ref.shape[0]))
    data = jnp.concatenate([ref[rows, :] for ref in time_refs], axis=1).astype(jnp.bfloat16)
    data = jnp.concatenate([data, data], axis=0)
    data = jnp.dot(table_ref[index], data, preferred_element_type=jnp.float32)
    return [(ref, (index,), data[:, k * LANES : (k + 1) * LANES]) for k, ref in enumerate(freq_refs)]


def back(table, coarse, freq_refs, time_refs, finish, index):
    rows = pl.ds(index, FINE, stride=pitch(coarse))
    data = jnp.concatenate([ref[index] for ref in freq_refs], axis=1)
    high = data.astype(jnp.bfloat16)
    low = (data - high.astype(jnp.float32)).astype(jnp.bfloat16)
    table = jnp.concatenate([table, table[:, : 2 * FINE]], axis=1)
    data = jnp.concatenate([high, high, low], axis=0)
    data = jnp.dot(table, data, preferred_element_type=jnp.float32)
    return [(ref, (rows,), part) for ref, part in zip(time_refs, finish(data[:, :LANES], data[:, LANES:]))]


def rows_of(index):
    start = pl.multiple_of(index * SLAB, SLAB)
    return pl.ds(start, SLAB), pl.ds(start + FINE, SLAB)


def load(freq_ref, index):
    real, imag = rows_of(index)
    return [(freq_ref[c, real, :], freq_ref[c, imag, :]) for c in range(freq_ref.shape[0])]


def stores(freq_ref, index, data):
    real, imag = rows_of(index)
    return [(freq_ref, (c, rows), part) for c, pair in enumerate(data) for rows, part in zip((real, imag), pair)]


def spectrum(freq_ref, index):
    return stores(freq_ref, index, fourier(load(freq_ref, index), -1))


def correlate(freq_ref, cot_ref, index):
    data, cot = load(freq_ref, index), load(cot_ref, index)
    products = [
        (br * cr + bi * ci, br * ci - bi * cr) for (br, bi), (cr, ci) in zip(fourier(data, -1), cot)
    ]
    return stores(freq_ref, index, fourier(products, 1))


def each(count, steps):
    def body(index, carry):
        for ref, where, value in [item for step in steps for item in step(index)]:
            ref[where] = value
        return carry

    lax.fori_loop(0, count, body, 0, unroll=min(UNROLL, count))


def gradients(forward_ref, inverse_ref, first_ref, times, freqs, fetch, finish):
    sig_time, cot_time, fil_time = times
    sig_freq, cot_freq, fil_freq = freqs
    coarse, slabs = forward_ref.shape[0], FINE // SLAB

    each(coarse, (lambda i: onward(forward_ref, (cot_time, fil_time), (cot_freq, fil_freq), i),))
    each(coarse, (lambda i: onward(forward_ref, (sig_time,), (sig_freq,), i),))
    each(slabs, (lambda i: spectrum(cot_freq, i),))
    each(slabs, (lambda i: correlate(fil_freq, cot_freq, i),))
    each(slabs, (lambda i: correlate(sig_freq, cot_freq, i),))
    fetch.wait()
    for index in range(coarse):
        table = inverse_ref[index] if index else first_ref[...]
        for ref, where, value in back(table, coarse, (fil_freq, sig_freq), times[:2], finish, index):
            ref[where] = value


def packed_core(forward_ref, inverse_ref, in_ref, out_ref, first_ref, arrived, *scratch):
    times, freqs = scratch[:3], scratch[3:]
    _, places, depth, _ = in_ref.shape
    rows = out_ref.shape[2]
    fetch = pltpu.make_async_copy(inverse_ref.at[0], first_ref, arrived)
    fetch.start()

    coarse = forward_ref.shape[0]
    groups = rows // coarse

    def span(place, group):
        return pl.ds(pl.multiple_of((place * groups + group) * pitch(coarse), 8), coarse)

    def unfold(place):
        first, second = in_ref[0, place, :rows, :], in_ref[1, place, :rows, :]
        folds = [in_ref[k, place, rows:, :] for k in range(2)]
        fil = jnp.concatenate([part for fold in folds for part in (merge(fold, fold), merge_right(fold, fold))], axis=0)
        for ref, data in zip(times, (merge(first, second), merge_right(first, second), fil)):
            data = data.astype(jnp.float32)
            for group in range(groups):
                ref[span(place, group), :] = data[group * coarse : (group + 1) * coarse]
        return ()

    def finish(sig, fil):
        left = left_lanes(sig.shape)
        fil = fil + pltpu.roll(fil, HALF, 1)
        return jnp.where(left, sig, fil), jnp.where(left, pltpu.roll(sig, HALF, 1), fil)

    def fold(place):
        for k in range(2):
            data = jnp.concatenate([times[k][span(place, group), :] for group in range(groups)], axis=0)
            out_ref[k, place] = data.astype(jnp.bfloat16)
        return ()

    each(places, (unfold,))
    gradients(forward_ref, inverse_ref, first_ref, times, freqs, fetch, finish)
    each(places, (fold,))


def plain_core(groups, forward_ref, inverse_ref, in_ref, out_ref, first_ref, arrived, *scratch):
    times, freqs = scratch[:3], scratch[3:]
    fetch = pltpu.make_async_copy(inverse_ref.at[0], first_ref, arrived)
    fetch.start()
    coarse = forward_ref.shape[0]

    def spans(group):
        return (
            pl.ds(pl.multiple_of(group * pitch(coarse), 8), coarse),
            pl.ds(pl.multiple_of(group * coarse, coarse), coarse),
        )

    def unfold(group):
        to, span = spans(group)
        return [(times[k], (to,), in_ref[k, span, :].astype(jnp.float32)) for k in range(3)]

    def finish(sig, fil):
        step = LANES // groups
        while step < LANES:
            fil, step = fil + pltpu.roll(fil, step, 1), 2 * step
        return sig, fil

    def fold(group):
        to, span = spans(group)
        return [(out_ref, (k, span), times[k][to, :].astype(jnp.bfloat16)) for k in range(2)]

    each(FINE, (unfold,))
    gradients(forward_ref, inverse_ref, first_ref, times, freqs, fetch, finish)
    each(FINE, (fold,))


def core(kernel, message, out_shape, total):
    coarse = total // FINE
    forward, inverse = tables(coarse)
    vmem = pl.BlockSpec(memory_space=pltpu.VMEM)
    return pl.pallas_call(
        kernel,
        in_specs=[vmem, vmem, vmem],
        out_specs=vmem,
        out_shape=pltpu.VMEM(out_shape, jnp.bfloat16),
        scratch_shapes=[pltpu.VMEM(inverse.shape[1:], jnp.bfloat16), pltpu.SemaphoreType.DMA]
        + [pltpu.VMEM(((FINE + 1) * pitch(coarse), LANES), jnp.float32)] * 3
        + [pltpu.VMEM((coarse, 2 * FINE, LANES), jnp.float32)] * 3,
        compiler_params=pltpu.CompilerParams(vmem_limit_bytes=total * 12 * 2**10),
        name="gradients",
    )(jnp.asarray(forward), jnp.asarray(inverse), pltpu.with_memory_space_constraint(message, pltpu.VMEM))


def exchange(message):
    return lax.all_to_all(message, both, split_axis=0, concat_axis=0, tiled=True)


def packed_body(signal, cotangent, long_filter):
    rows, columns = signal.shape
    places = lax.axis_size("cp")
    depth = rows + rows // 4
    hbm, vmem = pl.BlockSpec(memory_space=pltpu.HBM), pl.BlockSpec(memory_space=pltpu.VMEM)
    message = pl.pallas_call(
        pack_kernel,
        in_specs=[pl.BlockSpec(memory_space=pltpu.SMEM), hbm, hbm, hbm],
        out_specs=vmem,
        out_shape=pltpu.VMEM((2, places, depth, LANES), jnp.bfloat16),
        scratch_shapes=[
            pltpu.VMEM((rows, columns), jnp.bfloat16),
            pltpu.VMEM((rows, columns), jnp.bfloat16),
            pltpu.VMEM((rows // 2, columns), jnp.bfloat16),
            pltpu.SemaphoreType.DMA((3, IN_CHUNKS)),
        ],
        name="pack",
    )(lax.axis_index("tp").reshape(1), signal, cotangent, long_filter)
    message = exchange(message.reshape(2 * places, depth, LANES)).reshape(2, places, depth, LANES)
    message = core(packed_core, message, (2, places, rows, LANES), rows * places)
    message = exchange(message.reshape(2 * places, rows, LANES)).reshape(2, places, rows, LANES)
    return pl.pallas_call(
        unpack_kernel,
        in_specs=[vmem],
        out_specs=[hbm, hbm],
        out_shape=[jax.ShapeDtypeStruct((rows, columns), jnp.bfloat16)] * 2,
        scratch_shapes=[pltpu.VMEM((rows, columns), jnp.bfloat16)] * 2 + [pltpu.SemaphoreType.DMA((2, OUT_CHUNKS))],
        name="unpack",
    )(pltpu.with_memory_space_constraint(message, pltpu.VMEM))


def plain_body(signal, cotangent, long_filter):
    rows, columns = signal.shape
    groups, places = lax.axis_size("tp"), lax.axis_size("cp")
    total, width = rows * places, columns // (groups * places)

    def deal(block):
        return block.reshape(block.shape[0], groups * places, width).transpose(1, 0, 2).reshape(groups * places, -1)

    part = lax.axis_index("tp") * (rows // groups)
    share = lax.dynamic_slice_in_dim(long_filter, part, rows // groups, 0)
    message = exchange(jnp.concatenate([deal(signal), deal(cotangent), deal(share)], axis=1))
    sig, cot, fil = jnp.split(message, [rows * width, 2 * rows * width], axis=1)

    def arrange(block):
        block = block.reshape(groups, total, width).transpose(1, 0, 2)
        return jnp.pad(block, ((0, 0), (0, 0), (0, LANES // groups - width))).reshape(total, LANES)

    fil = fil.reshape(groups, places, rows // groups, width).transpose(1, 0, 2, 3).reshape(1, total, width)
    fil = jnp.broadcast_to(fil, (groups, total, width))
    data = jnp.stack([arrange(sig), arrange(cot), arrange(fil)])
    grads = core(functools.partial(plain_core, groups), data, (2, total, LANES), total)
    grads = grads.reshape(2, places, rows, groups, LANES // groups)[..., :width]
    message = exchange(grads.transpose(3, 1, 0, 2, 4).reshape(groups * places, 2 * rows * width))
    grads = message.reshape(groups * places, 2, rows, width).transpose(1, 2, 0, 3).reshape(2, rows, columns)
    return grads[0], grads[1]


def solution(mesh):
    groups, places = mesh.shape["tp"], mesh.shape["cp"]

    def body(signal, cotangent, long_filter):
        rows, columns = signal.shape
        packed = groups == 2 and columns == LANES * places and rows % 64 == 0
        return (packed_body if packed else plain_body)(signal, cotangent, long_filter)

    in_specs = (P("cp", "tp"), P("cp", "tp"), P("cp", None))
    out_specs = (P("cp", "tp"), P("cp", None))
    return jax.shard_map(body, mesh=mesh, in_specs=in_specs, out_specs=out_specs, check_vma=False)
```

```python
import functools
import math

import jax
import jax.numpy as jnp
import ml_dtypes
import numpy as np
from jax import lax
from jax.experimental import pallas as pl
from jax.experimental.pallas import tpu as pltpu
from jax.sharding import PartitionSpec as P

LANES = 128
FINE = 128
HALF = LANES // 2
SLAB = 8
UNROLL = 16
IN_CHUNKS = 2
OUT_CHUNKS = 4
both = ("tp", "cp")


def split(values):
    high = values.astype(ml_dtypes.bfloat16)
    low = (values - high.astype(np.float64)).astype(ml_dtypes.bfloat16)
    return high, low


def tables(coarse):
    total = coarse * FINE
    bins = np.arange(FINE, dtype=np.int64)[None, :, None]
    spots = coarse * np.arange(FINE, dtype=np.int64)[None, None, :] + np.arange(coarse, dtype=np.int64)[:, None, None]
    angle = ((4 * bins + 1) * spots % (4 * total)).astype(np.float64) * (2.0 * math.pi / (4 * total))
    table = np.concatenate([np.cos(angle), -np.sin(angle)], axis=1)
    forward = np.concatenate(split(table), axis=2)
    inverse = np.concatenate(split(table.transpose(0, 2, 1) / total), axis=2)
    return forward, inverse


def butterfly(even, odd, turn, size, sign):
    (er, ei), (dr, di) = even, odd
    if turn == 0:
        return (er + dr, ei + di), (er - dr, ei - di)
    if 4 * turn == size:
        back, forth = (er + di, ei - dr), (er - di, ei + dr)
        return (back, forth) if sign < 0 else (forth, back)
    if 8 * turn in (size, 3 * size):
        root = math.sqrt(0.5)
        total, gap = (dr + di) * root, ((di - dr) if sign < 0 else (dr - di)) * root
        if sign < 0 and 8 * turn == size:
            return (er + total, ei + gap), (er - total, ei - gap)
        if sign < 0:
            return (er + gap, ei - total), (er - gap, ei + total)
        if 8 * turn == size:
            return (er + gap, ei + total), (er - gap, ei - total)
        return (er - total, ei + gap), (er + total, ei - gap)
    cos, sin = math.cos(2 * math.pi * turn / size), sign * math.sin(2 * math.pi * turn / size)
    dr, di = dr * cos - di * sin, di * cos + dr * sin
    return (er + dr, ei + di), (er - dr, ei - di)


def fourier(data, sign):
    size = len(data)
    if size == 1:
        return data
    even, odd = fourier(data[0::2], sign), fourier(data[1::2], sign)
    pairs = [butterfly(even[turn], odd[turn], turn, size, sign) for turn in range(size // 2)]
    return [low for low, _ in pairs] + [high for _, high in pairs]


def left_lanes(shape):
    return lax.broadcasted_iota(jnp.int32, shape, 1) < HALF


def merge(left, right):
    return jnp.where(left_lanes(left.shape), left, pltpu.roll(right, HALF, 1))


def merge_right(left, right):
    return jnp.where(left_lanes(left.shape), pltpu.roll(left, HALF, 1), right)


def pack_kernel(part_ref, sig_hbm, cot_hbm, fil_hbm, out_ref, sig_ref, cot_ref, fil_ref, arrived):
    rows, columns = sig_ref.shape
    quarter = rows // 4
    start = pl.multiple_of(part_ref[0] * 2 * quarter, 2 * quarter)
    chunk = columns // IN_CHUNKS
    copies = []
    for c in range(IN_CHUNKS):
        lanes = pl.ds(c * chunk, chunk)
        copies.append(
            (
                pltpu.make_async_copy(sig_hbm.at[:, lanes], sig_ref.at[:, lanes], arrived.at[0, c]),
                pltpu.make_async_copy(cot_hbm.at[:, lanes], cot_ref.at[:, lanes], arrived.at[1, c]),
                pltpu.make_async_copy(
                    fil_hbm.at[pl.ds(start, 2 * quarter), lanes], fil_ref.at[:, lanes], arrived.at[2, c]
                ),
            )
        )
        for copy in copies[c]:
            copy.start()
    for c in range(IN_CHUNKS):
        for copy in copies[c]:
            copy.wait()
        for place in range(c * chunk // LANES, (c + 1) * chunk // LANES):
            lanes = pl.ds(place * LANES, LANES)
            sig, cot = sig_ref[:, lanes], cot_ref[:, lanes]
            out_ref[0, place, :rows, :] = merge(sig, cot)
            out_ref[1, place, :rows, :] = merge_right(sig, cot)
            top, bottom = fil_ref[:quarter, lanes], fil_ref[quarter:, lanes]
            out_ref[0, place, rows:, :] = merge(top, bottom)
            out_ref[1, place, rows:, :] = merge_right(top, bottom)


def unpack_kernel(in_ref, sig_hbm, fil_hbm, sig_ref, fil_ref, sent):
    columns = sig_ref.shape[1]
    chunk = columns // OUT_CHUNKS
    copies = []
    for c in range(OUT_CHUNKS):
        for place in range(c * chunk // LANES, (c + 1) * chunk // LANES):
            lanes = pl.ds(place * LANES, LANES)
            first, second = in_ref[0, place], in_ref[1, place]
            sig_ref[:, lanes] = merge(first, second)
            fil_ref[:, lanes] = merge_right(first, second)
        lanes = pl.ds(c * chunk, chunk)
        copies.append(pltpu.make_async_copy(sig_ref.at[:, lanes], sig_hbm.at[:, lanes], sent.at[0, c]))
        copies.append(pltpu.make_async_copy(fil_ref.at[:, lanes], fil_hbm.at[:, lanes], sent.at[1, c]))
        copies[-2].start()
        copies[-1].start()
    for copy in copies:
        copy.wait()


def pitch(coarse):
    return coarse + 8


def onward(table_ref, time_refs, freq_refs, index):
    rows = pl.ds(index, FINE, stride=pitch(table_ref.shape[0]))
    data = jnp.concatenate([ref[rows, :] for ref in time_refs], axis=1).astype(jnp.bfloat16)
    data = jnp.concatenate([data, data], axis=0)
    data = jnp.dot(table_ref[index], data, preferred_element_type=jnp.float32)
    return [(ref, (index,), data[:, k * LANES : (k + 1) * LANES]) for k, ref in enumerate(freq_refs)]


def back(table, coarse, freq_refs, time_refs, finish, index):
    rows = pl.ds(index, FINE, stride=pitch(coarse))
    data = jnp.concatenate([ref[index] for ref in freq_refs], axis=1)
    high = data.astype(jnp.bfloat16)
    low = (data - high.astype(jnp.float32)).astype(jnp.bfloat16)
    table = jnp.concatenate([table, table[:, : 2 * FINE]], axis=1)
    data = jnp.concatenate([high, high, low], axis=0)
    data = jnp.dot(table, data, preferred_element_type=jnp.float32)
    return [(ref, (rows,), part) for ref, part in zip(time_refs, finish(data[:, :LANES], data[:, LANES:]))]


def rows_of(index):
    start = pl.multiple_of(index * SLAB, SLAB)
    return pl.ds(start, SLAB), pl.ds(start + FINE, SLAB)


def load(freq_ref, index):
    real, imag = rows_of(index)
    return [(freq_ref[c, real, :], freq_ref[c, imag, :]) for c in range(freq_ref.shape[0])]


def stores(freq_ref, index, data):
    real, imag = rows_of(index)
    return [(freq_ref, (c, rows), part) for c, pair in enumerate(data) for rows, part in zip((real, imag), pair)]


def spectrum(freq_ref, index):
    return stores(freq_ref, index, fourier(load(freq_ref, index), -1))


def correlate(freq_ref, cot_ref, index):
    data, cot = load(freq_ref, index), load(cot_ref, index)
    products = [
        (br * cr + bi * ci, br * ci - bi * cr) for (br, bi), (cr, ci) in zip(fourier(data, -1), cot)
    ]
    return stores(freq_ref, index, fourier(products, 1))


def each(count, steps):
    def body(index, carry):
        for ref, where, value in [item for step in steps for item in step(index)]:
            ref[where] = value
        return carry

    lax.fori_loop(0, count, body, 0, unroll=min(UNROLL, count))


def gradients(forward_ref, inverse_ref, first_ref, times, freqs, fetch, finish):
    sig_time, cot_time, fil_time = times
    sig_freq, cot_freq, fil_freq = freqs
    coarse, slabs = forward_ref.shape[0], FINE // SLAB

    each(coarse, (lambda i: onward(forward_ref, (cot_time, fil_time), (cot_freq, fil_freq), i),))
    each(coarse, (lambda i: onward(forward_ref, (sig_time,), (sig_freq,), i),))
    each(slabs, (lambda i: spectrum(cot_freq, i),))
    each(slabs, (lambda i: correlate(fil_freq, cot_freq, i),))
    each(slabs, (lambda i: correlate(sig_freq, cot_freq, i),))
    fetch.wait()
    for index in range(coarse):
        table = inverse_ref[index] if index else first_ref[...]
        for ref, where, value in back(table, coarse, (fil_freq, sig_freq), times[:2], finish, index):
            ref[where] = value


def packed_core(forward_ref, inverse_ref, in_ref, out_ref, first_ref, arrived, *scratch):
    times, freqs = scratch[:3], scratch[3:]
    _, places, depth, _ = in_ref.shape
    rows = out_ref.shape[2]
    fetch = pltpu.make_async_copy(inverse_ref.at[0], first_ref, arrived)
    fetch.start()

    coarse = forward_ref.shape[0]
    groups = rows // coarse

    def span(place, group):
        return pl.ds(pl.multiple_of((place * groups + group) * pitch(coarse), 8), coarse)

    def unfold(place):
        first, second = in_ref[0, place, :rows, :], in_ref[1, place, :rows, :]
        folds = [in_ref[k, place, rows:, :] for k in range(2)]
        fil = jnp.concatenate([part for fold in folds for part in (merge(fold, fold), merge_right(fold, fold))], axis=0)
        for ref, data in zip(times, (merge(first, second), merge_right(first, second), fil)):
            data = data.astype(jnp.float32)
            for group in range(groups):
                ref[span(place, group), :] = data[group * coarse : (group + 1) * coarse]
        return ()

    def finish(sig, fil):
        fil = fil + pltpu.roll(fil, HALF, 1)
        return sig, fil

    def fold(place):
        sig, fil = (
            jnp.concatenate([ref[span(place, group), :] for group in range(groups)], axis=0).astype(jnp.bfloat16)
            for ref in times[:2]
        )
        left = left_lanes(sig.shape)
        out_ref[0, place] = jnp.where(left, sig, fil)
        out_ref[1, place] = jnp.where(left, pltpu.roll(sig, HALF, 1), fil)
        return ()

    each(places, (unfold,))
    gradients(forward_ref, inverse_ref, first_ref, times, freqs, fetch, finish)
    each(places, (fold,))


def plain_core(groups, forward_ref, inverse_ref, in_ref, out_ref, first_ref, arrived, *scratch):
    times, freqs = scratch[:3], scratch[3:]
    fetch = pltpu.make_async_copy(inverse_ref.at[0], first_ref, arrived)
    fetch.start()
    coarse = forward_ref.shape[0]

    def spans(group):
        return (
            pl.ds(pl.multiple_of(group * pitch(coarse), 8), coarse),
            pl.ds(pl.multiple_of(group * coarse, coarse), coarse),
        )

    def unfold(group):
        to, span = spans(group)
        return [(times[k], (to,), in_ref[k, span, :].astype(jnp.float32)) for k in range(3)]

    def finish(sig, fil):
        step = LANES // groups
        while step < LANES:
            fil, step = fil + pltpu.roll(fil, step, 1), 2 * step
        return sig, fil

    def fold(group):
        to, span = spans(group)
        return [(out_ref, (k, span), times[k][to, :].astype(jnp.bfloat16)) for k in range(2)]

    each(FINE, (unfold,))
    gradients(forward_ref, inverse_ref, first_ref, times, freqs, fetch, finish)
    each(FINE, (fold,))


def core(kernel, message, out_shape, total):
    coarse = total // FINE
    forward, inverse = tables(coarse)
    vmem = pl.BlockSpec(memory_space=pltpu.VMEM)
    return pl.pallas_call(
        kernel,
        in_specs=[vmem, vmem, vmem],
        out_specs=vmem,
        out_shape=pltpu.VMEM(out_shape, jnp.bfloat16),
        scratch_shapes=[pltpu.VMEM(inverse.shape[1:], jnp.bfloat16), pltpu.SemaphoreType.DMA]
        + [pltpu.VMEM(((FINE + 1) * pitch(coarse), LANES), jnp.float32)] * 3
        + [pltpu.VMEM((coarse, 2 * FINE, LANES), jnp.float32)] * 3,
        compiler_params=pltpu.CompilerParams(vmem_limit_bytes=total * 12 * 2**10),
        name="gradients",
    )(jnp.asarray(forward), jnp.asarray(inverse), pltpu.with_memory_space_constraint(message, pltpu.VMEM))


def exchange(message):
    return lax.all_to_all(message, both, split_axis=0, concat_axis=0, tiled=True)


def packed_body(signal, cotangent, long_filter):
    rows, columns = signal.shape
    places = lax.axis_size("cp")
    depth = rows + rows // 4
    hbm, vmem = pl.BlockSpec(memory_space=pltpu.HBM), pl.BlockSpec(memory_space=pltpu.VMEM)
    message = pl.pallas_call(
        pack_kernel,
        in_specs=[pl.BlockSpec(memory_space=pltpu.SMEM), hbm, hbm, hbm],
        out_specs=vmem,
        out_shape=pltpu.VMEM((2, places, depth, LANES), jnp.bfloat16),
        scratch_shapes=[
            pltpu.VMEM((rows, columns), jnp.bfloat16),
            pltpu.VMEM((rows, columns), jnp.bfloat16),
            pltpu.VMEM((rows // 2, columns), jnp.bfloat16),
            pltpu.SemaphoreType.DMA((3, IN_CHUNKS)),
        ],
        name="pack",
    )(lax.axis_index("tp").reshape(1), signal, cotangent, long_filter)
    message = exchange(message.reshape(2 * places, depth, LANES)).reshape(2, places, depth, LANES)
    message = core(packed_core, message, (2, places, rows, LANES), rows * places)
    message = exchange(message.reshape(2 * places, rows, LANES)).reshape(2, places, rows, LANES)
    return pl.pallas_call(
        unpack_kernel,
        in_specs=[vmem],
        out_specs=[hbm, hbm],
        out_shape=[jax.ShapeDtypeStruct((rows, columns), jnp.bfloat16)] * 2,
        scratch_shapes=[pltpu.VMEM((rows, columns), jnp.bfloat16)] * 2 + [pltpu.SemaphoreType.DMA((2, OUT_CHUNKS))],
        name="unpack",
    )(pltpu.with_memory_space_constraint(message, pltpu.VMEM))


def plain_body(signal, cotangent, long_filter):
    rows, columns = signal.shape
    groups, places = lax.axis_size("tp"), lax.axis_size("cp")
    total, width = rows * places, columns // (groups * places)

    def deal(block):
        return block.reshape(block.shape[0], groups * places, width).transpose(1, 0, 2).reshape(groups * places, -1)

    part = lax.axis_index("tp") * (rows // groups)
    share = lax.dynamic_slice_in_dim(long_filter, part, rows // groups, 0)
    message = exchange(jnp.concatenate([deal(signal), deal(cotangent), deal(share)], axis=1))
    sig, cot, fil = jnp.split(message, [rows * width, 2 * rows * width], axis=1)

    def arrange(block):
        block = block.reshape(groups, total, width).transpose(1, 0, 2)
        return jnp.pad(block, ((0, 0), (0, 0), (0, LANES // groups - width))).reshape(total, LANES)

    fil = fil.reshape(groups, places, rows // groups, width).transpose(1, 0, 2, 3).reshape(1, total, width)
    fil = jnp.broadcast_to(fil, (groups, total, width))
    data = jnp.stack([arrange(sig), arrange(cot), arrange(fil)])
    grads = core(functools.partial(plain_core, groups), data, (2, total, LANES), total)
    grads = grads.reshape(2, places, rows, groups, LANES // groups)[..., :width]
    message = exchange(grads.transpose(3, 1, 0, 2, 4).reshape(groups * places, 2 * rows * width))
    grads = message.reshape(groups * places, 2, rows, width).transpose(1, 2, 0, 3).reshape(2, rows, columns)
    return grads[0], grads[1]


def solution(mesh):
    groups, places = mesh.shape["tp"], mesh.shape["cp"]

    def body(signal, cotangent, long_filter):
        rows, columns = signal.shape
        packed = groups == 2 and columns == LANES * places and rows % 64 == 0
        return (packed_body if packed else plain_body)(signal, cotangent, long_filter)

    in_specs = (P("cp", "tp"), P("cp", "tp"), P("cp", None))
    out_specs = (P("cp", "tp"), P("cp", None))
    return jax.shard_map(body, mesh=mesh, in_specs=in_specs, out_specs=out_specs, check_vma=False)
```

```python
import functools
import math

import jax
import jax.numpy as jnp
import ml_dtypes
import numpy as np
from jax import lax
from jax.experimental import pallas as pl
from jax.experimental.pallas import tpu as pltpu
from jax.sharding import PartitionSpec as P

LANES = 128
FINE = 128
HALF = LANES // 2
SLAB = 8
UNROLL = 16
IN_CHUNKS = 2
OUT_CHUNKS = 4
both = ("tp", "cp")


def split(values):
    high = values.astype(ml_dtypes.bfloat16)
    low = (values - high.astype(np.float64)).astype(ml_dtypes.bfloat16)
    return high, low


def tables(coarse):
    total = coarse * FINE
    bins = np.arange(FINE, dtype=np.int64)[None, :, None]
    spots = coarse * np.arange(FINE, dtype=np.int64)[None, None, :] + np.arange(coarse, dtype=np.int64)[:, None, None]
    angle = ((4 * bins + 1) * spots % (4 * total)).astype(np.float64) * (2.0 * math.pi / (4 * total))
    table = np.concatenate([np.cos(angle), -np.sin(angle)], axis=1)
    forward = np.concatenate(split(table), axis=2)
    inverse = np.concatenate(split(table.transpose(0, 2, 1) / total), axis=2)
    return forward, inverse


def butterfly(even, odd, turn, size, sign):
    (er, ei), (dr, di) = even, odd
    if turn == 0:
        return (er + dr, ei + di), (er - dr, ei - di)
    if 4 * turn == size:
        back, forth = (er + di, ei - dr), (er - di, ei + dr)
        return (back, forth) if sign < 0 else (forth, back)
    if 8 * turn in (size, 3 * size):
        root = math.sqrt(0.5)
        total, gap = (dr + di) * root, ((di - dr) if sign < 0 else (dr - di)) * root
        if sign < 0 and 8 * turn == size:
            return (er + total, ei + gap), (er - total, ei - gap)
        if sign < 0:
            return (er + gap, ei - total), (er - gap, ei + total)
        if 8 * turn == size:
            return (er + gap, ei + total), (er - gap, ei - total)
        return (er - total, ei + gap), (er + total, ei - gap)
    cos, sin = math.cos(2 * math.pi * turn / size), sign * math.sin(2 * math.pi * turn / size)
    dr, di = dr * cos - di * sin, di * cos + dr * sin
    return (er + dr, ei + di), (er - dr, ei - di)


def fourier(data, sign):
    size = len(data)
    if size == 1:
        return data
    even, odd = fourier(data[0::2], sign), fourier(data[1::2], sign)
    pairs = [butterfly(even[turn], odd[turn], turn, size, sign) for turn in range(size // 2)]
    return [low for low, _ in pairs] + [high for _, high in pairs]


def left_lanes(shape):
    return lax.broadcasted_iota(jnp.int32, shape, 1) < HALF


def merge(left, right):
    return jnp.where(left_lanes(left.shape), left, pltpu.roll(right, HALF, 1))


def merge_right(left, right):
    return jnp.where(left_lanes(left.shape), pltpu.roll(left, HALF, 1), right)


def pack_kernel(part_ref, sig_hbm, cot_hbm, fil_hbm, out_ref, sig_ref, cot_ref, fil_ref, arrived):
    rows, columns = sig_ref.shape
    quarter = rows // 4
    start = pl.multiple_of(part_ref[0] * 2 * quarter, 2 * quarter)
    chunk = columns // IN_CHUNKS
    copies = []
    share = pltpu.make_async_copy(fil_hbm.at[pl.ds(start, 2 * quarter)], fil_ref, arrived.at[2, 0])
    share.start()
    for c in range(IN_CHUNKS):
        lanes = pl.ds(c * chunk, chunk)
        copies.append(
            (
                pltpu.make_async_copy(sig_hbm.at[:, lanes], sig_ref.at[:, lanes], arrived.at[0, c]),
                pltpu.make_async_copy(cot_hbm.at[:, lanes], cot_ref.at[:, lanes], arrived.at[1, c]),
            )
        )
        for copy in copies[c]:
            copy.start()
    share.wait()
    for place in range(columns // LANES):
        lanes = pl.ds(place * LANES, LANES)
        top, bottom = fil_ref[:quarter, lanes], fil_ref[quarter:, lanes]
        out_ref[0, place, rows:, :] = merge(top, bottom)
        out_ref[1, place, rows:, :] = merge_right(top, bottom)
    for c in range(IN_CHUNKS):
        for copy in copies[c]:
            copy.wait()
        for place in range(c * chunk // LANES, (c + 1) * chunk // LANES):
            lanes = pl.ds(place * LANES, LANES)
            sig, cot = sig_ref[:, lanes], cot_ref[:, lanes]
            out_ref[0, place, :rows, :] = merge(sig, cot)
            out_ref[1, place, :rows, :] = merge_right(sig, cot)


def unpack_kernel(in_ref, sig_hbm, fil_hbm, sig_ref, fil_ref, sent):
    columns = sig_ref.shape[1]
    chunk = columns // OUT_CHUNKS
    copies = []
    for c in range(OUT_CHUNKS):
        for place in range(c * chunk // LANES, (c + 1) * chunk // LANES):
            lanes = pl.ds(place * LANES, LANES)
            first, second = in_ref[0, place], in_ref[1, place]
            sig_ref[:, lanes] = merge(first, second)
            fil_ref[:, lanes] = merge_right(first, second)
        lanes = pl.ds(c * chunk, chunk)
        copies.append(pltpu.make_async_copy(sig_ref.at[:, lanes], sig_hbm.at[:, lanes], sent.at[0, c]))
        copies.append(pltpu.make_async_copy(fil_ref.at[:, lanes], fil_hbm.at[:, lanes], sent.at[1, c]))
        copies[-2].start()
        copies[-1].start()
    for copy in copies:
        copy.wait()


def pitch(coarse):
    return coarse + 8


def onward(table_ref, time_refs, freq_refs, index):
    rows = pl.ds(index, FINE, stride=pitch(table_ref.shape[0]))
    data = jnp.concatenate([ref[rows, :] for ref in time_refs], axis=1).astype(jnp.bfloat16)
    data = jnp.concatenate([data, data], axis=0)
    data = jnp.dot(table_ref[index], data, preferred_element_type=jnp.float32)
    return [(ref, (index,), data[:, k * LANES : (k + 1) * LANES]) for k, ref in enumerate(freq_refs)]


def back(table, coarse, freq_refs, time_refs, finish, index):
    rows = pl.ds(index, FINE, stride=pitch(coarse))
    data = jnp.concatenate([ref[index] for ref in freq_refs], axis=1)
    high = data.astype(jnp.bfloat16)
    low = (data - high.astype(jnp.float32)).astype(jnp.bfloat16)
    table = jnp.concatenate([table, table[:, : 2 * FINE]], axis=1)
    data = jnp.concatenate([high, high, low], axis=0)
    data = jnp.dot(table, data, preferred_element_type=jnp.float32)
    return [(ref, (rows,), part) for ref, part in zip(time_refs, finish(data[:, :LANES], data[:, LANES:]))]


def rows_of(index):
    start = pl.multiple_of(index * SLAB, SLAB)
    return pl.ds(start, SLAB), pl.ds(start + FINE, SLAB)


def load(freq_ref, index):
    real, imag = rows_of(index)
    return [(freq_ref[c, real, :], freq_ref[c, imag, :]) for c in range(freq_ref.shape[0])]


def stores(freq_ref, index, data):
    real, imag = rows_of(index)
    return [(freq_ref, (c, rows), part) for c, pair in enumerate(data) for rows, part in zip((real, imag), pair)]


def spectrum(freq_ref, index):
    return stores(freq_ref, index, fourier(load(freq_ref, index), -1))


def correlate(freq_ref, cot_ref, index):
    data, cot = load(freq_ref, index), load(cot_ref, index)
    products = [
        (br * cr + bi * ci, br * ci - bi * cr) for (br, bi), (cr, ci) in zip(fourier(data, -1), cot)
    ]
    return stores(freq_ref, index, fourier(products, 1))


def each(count, steps):
    def body(index, carry):
        for ref, where, value in [item for step in steps for item in step(index)]:
            ref[where] = value
        return carry

    lax.fori_loop(0, count, body, 0, unroll=min(UNROLL, count))


def gradients(forward_ref, inverse_ref, first_ref, times, freqs, fetch, finish):
    sig_time, cot_time, fil_time = times
    sig_freq, cot_freq, fil_freq = freqs
    coarse, slabs = forward_ref.shape[0], FINE // SLAB

    each(coarse, (lambda i: onward(forward_ref, (cot_time, fil_time), (cot_freq, fil_freq), i),))
    each(coarse, (lambda i: onward(forward_ref, (sig_time,), (sig_freq,), i),))
    each(slabs, (lambda i: spectrum(cot_freq, i),))
    each(slabs, (lambda i: correlate(fil_freq, cot_freq, i),))
    each(slabs, (lambda i: correlate(sig_freq, cot_freq, i),))
    fetch.wait()
    for index in range(coarse):
        table = inverse_ref[index] if index else first_ref[...]
        for ref, where, value in back(table, coarse, (fil_freq, sig_freq), times[:2], finish, index):
            ref[where] = value


def packed_core(forward_ref, inverse_ref, in_ref, out_ref, first_ref, arrived, *scratch):
    times, freqs = scratch[:3], scratch[3:]
    _, places, depth, _ = in_ref.shape
    rows = out_ref.shape[2]
    fetch = pltpu.make_async_copy(inverse_ref.at[0], first_ref, arrived)
    fetch.start()

    coarse = forward_ref.shape[0]
    groups = rows // coarse

    def span(place, group):
        return pl.ds(pl.multiple_of((place * groups + group) * pitch(coarse), 8), coarse)

    def unfold(place):
        first, second = in_ref[0, place, :rows, :], in_ref[1, place, :rows, :]
        folds = [in_ref[k, place, rows:, :] for k in range(2)]
        fil = jnp.concatenate([part for fold in folds for part in (merge(fold, fold), merge_right(fold, fold))], axis=0)
        for ref, data in zip(times, (merge(first, second), merge_right(first, second), fil)):
            data = data.astype(jnp.float32)
            for group in range(groups):
                ref[span(place, group), :] = data[group * coarse : (group + 1) * coarse]
        return ()

    def finish(sig, fil):
        fil = fil + pltpu.roll(fil, HALF, 1)
        return sig, fil

    def fold(place):
        sig, fil = (
            jnp.concatenate([ref[span(place, group), :] for group in range(groups)], axis=0).astype(jnp.bfloat16)
            for ref in times[:2]
        )
        left = left_lanes(sig.shape)
        out_ref[0, place] = jnp.where(left, sig, fil)
        out_ref[1, place] = jnp.where(left, pltpu.roll(sig, HALF, 1), fil)
        return ()

    each(places, (unfold,))
    gradients(forward_ref, inverse_ref, first_ref, times, freqs, fetch, finish)
    each(places, (fold,))


def plain_core(groups, forward_ref, inverse_ref, in_ref, out_ref, first_ref, arrived, *scratch):
    times, freqs = scratch[:3], scratch[3:]
    fetch = pltpu.make_async_copy(inverse_ref.at[0], first_ref, arrived)
    fetch.start()
    coarse = forward_ref.shape[0]

    def spans(group):
        return (
            pl.ds(pl.multiple_of(group * pitch(coarse), 8), coarse),
            pl.ds(pl.multiple_of(group * coarse, coarse), coarse),
        )

    def unfold(group):
        to, span = spans(group)
        return [(times[k], (to,), in_ref[k, span, :].astype(jnp.float32)) for k in range(3)]

    def finish(sig, fil):
        step = LANES // groups
        while step < LANES:
            fil, step = fil + pltpu.roll(fil, step, 1), 2 * step
        return sig, fil

    def fold(group):
        to, span = spans(group)
        return [(out_ref, (k, span), times[k][to, :].astype(jnp.bfloat16)) for k in range(2)]

    each(FINE, (unfold,))
    gradients(forward_ref, inverse_ref, first_ref, times, freqs, fetch, finish)
    each(FINE, (fold,))


def core(kernel, message, out_shape, total):
    coarse = total // FINE
    forward, inverse = tables(coarse)
    vmem = pl.BlockSpec(memory_space=pltpu.VMEM)
    return pl.pallas_call(
        kernel,
        in_specs=[vmem, vmem, vmem],
        out_specs=vmem,
        out_shape=pltpu.VMEM(out_shape, jnp.bfloat16),
        scratch_shapes=[pltpu.VMEM(inverse.shape[1:], jnp.bfloat16), pltpu.SemaphoreType.DMA]
        + [pltpu.VMEM(((FINE + 1) * pitch(coarse), LANES), jnp.float32)] * 3
        + [pltpu.VMEM((coarse, 2 * FINE, LANES), jnp.float32)] * 3,
        compiler_params=pltpu.CompilerParams(vmem_limit_bytes=total * 12 * 2**10),
        name="gradients",
    )(jnp.asarray(forward), jnp.asarray(inverse), pltpu.with_memory_space_constraint(message, pltpu.VMEM))


def exchange(message):
    return lax.all_to_all(message, both, split_axis=0, concat_axis=0, tiled=True)


def packed_body(signal, cotangent, long_filter):
    rows, columns = signal.shape
    places = lax.axis_size("cp")
    depth = rows + rows // 4
    hbm, vmem = pl.BlockSpec(memory_space=pltpu.HBM), pl.BlockSpec(memory_space=pltpu.VMEM)
    message = pl.pallas_call(
        pack_kernel,
        in_specs=[pl.BlockSpec(memory_space=pltpu.SMEM), hbm, hbm, hbm],
        out_specs=vmem,
        out_shape=pltpu.VMEM((2, places, depth, LANES), jnp.bfloat16),
        scratch_shapes=[
            pltpu.VMEM((rows, columns), jnp.bfloat16),
            pltpu.VMEM((rows, columns), jnp.bfloat16),
            pltpu.VMEM((rows // 2, columns), jnp.bfloat16),
            pltpu.SemaphoreType.DMA((3, IN_CHUNKS)),
        ],
        name="pack",
    )(lax.axis_index("tp").reshape(1), signal, cotangent, long_filter)
    message = exchange(message.reshape(2 * places, depth, LANES)).reshape(2, places, depth, LANES)
    message = core(packed_core, message, (2, places, rows, LANES), rows * places)
    message = exchange(message.reshape(2 * places, rows, LANES)).reshape(2, places, rows, LANES)
    return pl.pallas_call(
        unpack_kernel,
        in_specs=[vmem],
        out_specs=[hbm, hbm],
        out_shape=[jax.ShapeDtypeStruct((rows, columns), jnp.bfloat16)] * 2,
        scratch_shapes=[pltpu.VMEM((rows, columns), jnp.bfloat16)] * 2 + [pltpu.SemaphoreType.DMA((2, OUT_CHUNKS))],
        name="unpack",
    )(pltpu.with_memory_space_constraint(message, pltpu.VMEM))


def plain_body(signal, cotangent, long_filter):
    rows, columns = signal.shape
    groups, places = lax.axis_size("tp"), lax.axis_size("cp")
    total, width = rows * places, columns // (groups * places)

    def deal(block):
        return block.reshape(block.shape[0], groups * places, width).transpose(1, 0, 2).reshape(groups * places, -1)

    part = lax.axis_index("tp") * (rows // groups)
    share = lax.dynamic_slice_in_dim(long_filter, part, rows // groups, 0)
    message = exchange(jnp.concatenate([deal(signal), deal(cotangent), deal(share)], axis=1))
    sig, cot, fil = jnp.split(message, [rows * width, 2 * rows * width], axis=1)

    def arrange(block):
        block = block.reshape(groups, total, width).transpose(1, 0, 2)
        return jnp.pad(block, ((0, 0), (0, 0), (0, LANES // groups - width))).reshape(total, LANES)

    fil = fil.reshape(groups, places, rows // groups, width).transpose(1, 0, 2, 3).reshape(1, total, width)
    fil = jnp.broadcast_to(fil, (groups, total, width))
    data = jnp.stack([arrange(sig), arrange(cot), arrange(fil)])
    grads = core(functools.partial(plain_core, groups), data, (2, total, LANES), total)
    grads = grads.reshape(2, places, rows, groups, LANES // groups)[..., :width]
    message = exchange(grads.transpose(3, 1, 0, 2, 4).reshape(groups * places, 2 * rows * width))
    grads = message.reshape(groups * places, 2, rows, width).transpose(1, 2, 0, 3).reshape(2, rows, columns)
    return grads[0], grads[1]


def solution(mesh):
    groups, places = mesh.shape["tp"], mesh.shape["cp"]

    def body(signal, cotangent, long_filter):
        rows, columns = signal.shape
        packed = groups == 2 and columns == LANES * places and rows % 64 == 0
        return (packed_body if packed else plain_body)(signal, cotangent, long_filter)

    in_specs = (P("cp", "tp"), P("cp", "tp"), P("cp", None))
    out_specs = (P("cp", "tp"), P("cp", None))
    return jax.shard_map(body, mesh=mesh, in_specs=in_specs, out_specs=out_specs, check_vma=False)
```
